128 devices in a mesh: gx: 8 (over x, core), gy: 16 (over y, z).
Axes of the slice: x: 4, y: 4, z: 4, core: 2. Of those that a mesh axis runs over, the one named last changes fastest.
Arguments:
- coverage: int32 [8192, 8192], P('gx', 'gy'), may hold values from 0 to 64, as said below
- dose: float32 [8192, 8192], P('gx', 'gy'), may hold values from 0.5 to 2, as said below
Outputs:
- dose_map: float32 [8192, 8192], P('gx', 'gy')
- residual: float32 [8192, 8192], P('gx', 'gy')
The draws below stay inside these ranges and needn't reach their ends.
Inputs may be any that keep to these rules, and one draw needn't show every extreme that they name: coverage counts 64ths of a cell's area. `dose`: doses are positive.
All inputs are finite; a program needn't handle non-finite values.
Results may differ from the reference program's by a relative error of at most 0.0001.
Values sent between devices are 32-bit elements; how exact they have to be, the bound alone decides.
A program may use at most 64 MiB of HBM per device.

```python
import math
import jax
import jax.numpy as jnp
from jax import lax

RIM = 30
COARSE = 1024
FOG = 3072
ITERS = 6
NX = 8192
NY = 8192


def draw_coverage(key, part):
    key = jax.random.fold_in(key, 7)
    span = 48
    rows_region = NX // span + 1
    cols_region = NY // span + 1
    keys = jax.random.split(key, 8)
    region_shape = (rows_region, cols_region)
    block_shape = (NX // COARSE, NY // COARSE)
    kind = jax.random.randint(keys[0], region_shape, 0, 6)
    kind = kind.at[0, 0].set(2)
    period = jax.random.randint(keys[1], region_shape, 4, 25)
    width_raw = jax.random.randint(keys[2], region_shape, 1, 24)
    width = 1 + (width_raw - 1) % (period - 1)
    level = jax.random.randint(keys[3], region_shape, 8, 57)
    speckle = jax.random.randint(keys[4], (NX, NY), 0, 65)
    sparse_share = jax.random.randint(keys[5], block_shape, 0, 8)
    keep_draw = jax.random.randint(keys[6], region_shape, 0, 8)
    keep_draw = keep_draw.at[0, 0].set(7)
    block_scale = jax.random.randint(keys[7], block_shape, 4, 65)
    block_scale = block_scale.at[0, 0].set(64)
    row_index = jnp.arange(NX)[:, None]
    col_index = jnp.arange(NY)[None, :]
    region_row = row_index // span
    region_col = col_index // span
    kind_cell = kind[region_row, region_col]
    period_cell = period[region_row, region_col]
    width_cell = width[region_row, region_col]
    level_cell = level[region_row, region_col]
    keep_cell = keep_draw[region_row, region_col]
    sparse_cell = sparse_share[row_index // COARSE, col_index // COARSE]
    scale_cell = block_scale[row_index // COARSE, col_index // COARSE]
    full_cell = jnp.full((NX, NY), 64, jnp.int32)
    empty_cell = jnp.zeros((NX, NY), jnp.int32)
    lines_first = jnp.where(row_index % period_cell < width_cell, 64, 0)
    lines_second = jnp.where(col_index % period_cell < width_cell, 64, 0)
    layout = jnp.select([kind_cell == 0, kind_cell == 1, kind_cell == 2, kind_cell == 3, kind_cell == 4], [empty_cell, full_cell, lines_first, lines_second, level_cell], speckle)
    layout = jnp.where(keep_cell < sparse_cell, 0, layout)
    layout = layout * scale_cell // 64
    return layout.astype(jnp.int32)


def draw_dose(key, part):
    key = jax.random.fold_in(key, 11)
    keys = jax.random.split(key, 2)
    block_shape = (NX // COARSE, NY // COARSE)
    reach = math.log(2.0)
    block_level = jax.random.uniform(keys[0], block_shape, jnp.float32, -reach, reach)
    cell_level = jax.random.uniform(keys[1], (NX, NY), jnp.float32, -reach, reach)
    row_index = jnp.arange(NX)[:, None] // COARSE
    col_index = jnp.arange(NY)[None, :] // COARSE
    exponent = 0.7 * block_level[row_index, col_index] + 0.3 * cell_level
    return jnp.exp(exponent).astype(jnp.float32)


def setup_inputs(seed: int = 0) -> dict:
    key_of = jax.random.split(jax.random.key(seed), 3)
    return {
        "coverage": draw_coverage(jax.random.fold_in(key_of[2], 71), 0),
        "dose": draw_dose(jax.random.fold_in(key_of[2], 71), 0),
    }


def back_kernel():
    offsets = jnp.arange(-RIM, RIM + 1).astype(jnp.float32)
    weights = jnp.exp(-offsets * offsets / 200.0)
    return weights / jnp.sum(weights)

def fog_matrix(length):
    sigma = FOG / COARSE
    first = jnp.arange(length).astype(jnp.float32)[:, None]
    second = jnp.arange(length).astype(jnp.float32)[None, :]
    spread = first - second
    return jnp.exp(-spread * spread / (2.0 * sigma * sigma)) / (math.sqrt(2.0 * math.pi) * sigma)

def blur(charge):
    kernel = back_kernel()
    image = charge[None, None]
    along_first = lax.conv_general_dilated(image, kernel.reshape(1, 1, -1, 1), (1, 1), ((RIM, RIM), (0, 0)), precision=lax.Precision.HIGHEST)
    both_ways = lax.conv_general_dilated(along_first, kernel.reshape(1, 1, 1, -1), (1, 1), ((0, 0), (RIM, RIM)), precision=lax.Precision.HIGHEST)
    return both_ways[0, 0]

def reference(coverage, dose):
    fraction = coverage.astype(jnp.float32) / 64.0
    rows_coarse = NX // COARSE
    cols_coarse = NY // COARSE
    fog_first = fog_matrix(rows_coarse)
    fog_second = fog_matrix(cols_coarse)
    dose_map = dose
    residual = jnp.zeros_like(dose)
    for step in range(ITERS):
        charge = fraction * dose_map
        back = blur(charge)
        coarse = charge.reshape(rows_coarse, COARSE, cols_coarse, COARSE).mean(axis=(1, 3))
        fog = jnp.dot(jnp.dot(fog_first, coarse, precision=lax.Precision.HIGHEST), fog_second.T, precision=lax.Precision.HIGHEST)
        fog_fine = jnp.broadcast_to(fog[:, None, :, None], (rows_coarse, COARSE, cols_coarse, COARSE)).reshape(NX, NY)
        energy = (charge + 0.7 * back + 0.3 * fog_fine) / 2.0
        residual = 0.5 - energy
        dose_map = dose_map + 1.5 * residual
    return (dose_map, residual)
```

```python
import functools
import math

import jax
import jax.numpy as jnp
import numpy as np
from jax import lax
from jax.experimental import pallas as pl
from jax.experimental.pallas import tpu as pltpu
from jax.sharding import PartitionSpec as P

RIM = 30
PAD = 32
COARSE = 1024
FOG = 3072
ITERS = 6
RB = 256
CB = 256
BF = jnp.bfloat16
F32 = jnp.float32
MESH = pl.DeviceIdType.MESH


def two_terms(x):
    hi = np.asarray(x, np.float32).astype(BF)
    lo = (x - hi.astype(np.float64)).astype(np.float32).astype(BF)
    return hi, lo


def taps():
    k = np.arange(-RIM, RIM + 1).astype(np.float64)
    w = np.exp(-k * k / 200.0)
    return w / w.sum()


def band_first():
    w = taps()
    band = np.zeros((RB, RB + 2 * PAD))
    for i in range(RB):
        band[i, i + PAD - RIM : i + PAD + RIM + 1] = w
    hi, lo = two_terms(band)
    return np.concatenate([hi, lo, hi], axis=1)


def band_second():
    w = 0.525 * taps()

    def weight(c, j):
        return w[c - j + RIM] if abs(c - j) <= RIM else 0.0

    main = np.array([[weight(c, j) for j in range(CB)] for c in range(CB)])
    beside = [c for c in range(-PAD, 0)] + [c for c in range(CB, CB + PAD)]
    side = np.array([[weight(c, j) for j in range(CB)] for c in beside])
    mh, ml = two_terms(main)
    sh, sl = two_terms(side)
    return np.concatenate([mh, ml, mh, sh, sh, sl, np.zeros_like(sl)], axis=0)


def fog_matrix(n):
    s = FOG / COARSE
    k = np.arange(n).astype(np.float64)
    spread = k[:, None] - k[None, :]
    return np.exp(-spread * spread / (2.0 * s * s)) / (math.sqrt(2.0 * math.pi) * s)


def split(x):
    hi = x.astype(BF)
    return hi, (x - hi.astype(F32)).astype(BF)


def wide(row):
    return jnp.concatenate([row, row], axis=1)


def kernel(ngx, ngy, cover_hbm, dose_hbm, a1_hbm, w2_hbm, qc_hbm, pc_hbm, out_d, out_r,
           cover, d, f, u, a1, w2, qc, pc, chi, clo, vhi, vlo, vmix, acc, gbuf, fsum,
           rsend, rrecv, csend, crecv, krecv, frs, frr, fcs, fcr, fkr, asend, arecv, bsend, brecv,
           in_sem, out_sem, row_s, row_r, col_s, col_r, cor_s, cor_r,
           frow_s, frow_r, fcol_s, fcol_r, fcor_s, fcor_r, fa_s, fa_r, fb_s, fb_r):
    height, breadth = d.shape
    nb = height // RB
    nt = breadth // CB
    per = COARSE // breadth
    ni, nj = ngx * height // COARSE, ngy * breadth // COARSE
    i, j = lax.axis_index("gx"), lax.axis_index("gy")
    step_x = (lax.rem(i + ngx - 1, ngx), lax.rem(i + 1, ngx))
    step_y = (lax.rem(j + ngy - 1, ngy), lax.rem(j + 1, ngy))
    has_x = (i > 0, i < ngx - 1)
    has_y = (j > 0, j < ngy - 1)
    blk_j = j // per
    side_j = (jnp.maximum(j - 1, 0) // per, jnp.minimum(j + 1, ngy - 1) // per)
    edge = (0, breadth - 128)

    def dev(x, y):
        return {"gx": x, "gy": y}

    def remote(src, dst, ss, rs, to):
        return pltpu.make_async_remote_copy(
            src_ref=src, dst_ref=dst, send_sem=ss, recv_sem=rs, device_id=to, device_id_type=MESH
        )

    def row_copy(v, par):
        return remote(rsend.at[v], rrecv.at[par, 1 - v], row_s.at[v], row_r.at[par, 1 - v],
                      dev(step_x[v], j))

    def row_wait(v, par):
        remote(rsend.at[v], rrecv.at[par, v], row_s.at[v], row_r.at[par, v], dev(step_x[v], j)).wait_recv()

    def col_copy(h, r, par):
        return remote(csend.at[h, r], crecv.at[par, 1 - h, r], col_s.at[h, r],
                      col_r.at[par, 1 - h, r], dev(i, step_y[h]))

    def col_wait(h, r, par):
        remote(csend.at[h, r], crecv.at[par, h, r], col_s.at[h, r], col_r.at[par, h, r],
               dev(i, step_y[h])).wait_recv()

    def cor_copy(v, h, par):
        return remote(rsend.at[v, :, pl.ds(edge[h], 128)], krecv.at[par, 1 - v, 1 - h],
                      cor_s.at[v, h], cor_r.at[par, 1 - v, 1 - h], dev(step_x[v], step_y[h]))

    def cor_wait(v, h, par):
        remote(rsend.at[v, :, pl.ds(edge[h], 128)], krecv.at[par, v, h],
               cor_s.at[v, h], cor_r.at[par, v, h], dev(step_x[v], step_y[h])).wait_recv()

    def frow_copy(v, slot):
        return remote(frs.at[v], frr.at[slot], frow_s.at[v], frow_r.at[slot], dev(step_x[v], j))

    def fcol_copy(h, slot):
        return remote(fcs.at[h], fcr.at[slot], fcol_s.at[h], fcol_r.at[slot], dev(i, step_y[h]))

    def fcor_copy(v, h, sv, sh):
        return remote(frs.at[v, :, pl.ds(edge[h], 128)], fkr.at[sv, sh], fcor_s.at[v, h],
                      fcor_r.at[sv, sh], dev(step_x[v], step_y[h]))

    def share_copy(o, par, slot):
        return remote(asend, arecv.at[par, slot], fa_s.at[o], fa_r.at[par, slot],
                      dev(i, lax.rem(j + o, ngy)))

    def fog_copy(o, par, slot):
        return remote(bsend, brecv.at[par, slot], fb_s.at[o], fb_r.at[par, slot],
                      dev(lax.rem(i + o, ngx), j))

    lane = lax.broadcasted_iota(jnp.int32, (64, 128), 1)
    lane_rb = lax.broadcasted_iota(jnp.int32, (RB, 128), 1)
    lane_pad = lax.broadcasted_iota(jnp.int32, (PAD, 128), 1)
    lane1 = lax.broadcasted_iota(jnp.int32, (1, 128), 1)
    lane_mix = lax.rem(lax.broadcasted_iota(jnp.int32, (RB, 256), 1), 128) < 64

    def roll(x, shift):
        shift = shift % 128
        return x if shift == 0 else pltpu.roll(x, shift, 1)

    def pack(tile, first_lane):
        parts = [roll(tile[64 * q : 64 * q + 64], 32 * q - first_lane) for q in range(4)]
        low = jnp.where(lane < 32, parts[0], parts[1])
        high = jnp.where(lane < 96, parts[2], parts[3])
        return jnp.where(lane < 64, low, high)

    def unpack(piece, first_lane):
        return jnp.concatenate([roll(piece, first_lane - 32 * q) for q in range(4)], axis=0)

    def put_side(rows, c1, c2, left, right, lanes):
        e0 = jnp.where(lanes < 32, left, roll(c2, 32))
        e1 = jnp.where(lanes < 32, roll(c1, 32), right)
        for n, e in enumerate((e0, e1)):
            hi, lo = split(jnp.where(lanes < 64, e, roll(e, 64)))
            cs = slice(breadth + 128 * n, breadth + 128 * n + 128)
            chi[rows, cs] = hi
            if lo is not None:
                clo[rows, cs] = lo

    def first_dot(r, n):
        rows = slice(r * RB, r * RB + RB + 2 * PAD)
        cs = slice(n * CB, n * CB + CB)
        hi = chi[rows, cs]
        return jnp.dot(a1[...], jnp.concatenate([hi, hi, clo[rows, cs]], axis=0),
                       preferred_element_type=F32)

    def first_main(r):
        for n in range(nt):
            hi, lo = split(first_dot(r, n))
            vhi[r * RB : r * RB + RB, n * CB : n * CB + CB] = hi
            vlo[r * RB : r * RB + RB, n * CB : n * CB + CB] = lo

    def put_mix(r, v):
        hi = v.astype(BF).astype(F32)
        vmix[r * RB : r * RB + RB, :] = jnp.where(lane_mix, hi, v - hi).astype(BF)

    def second_dot(r, t):
        rows = slice(r * RB, r * RB + RB)
        hi = vhi[rows, t * CB : t * CB + CB]
        mix = vmix[rows, t * 128 : t * 128 + 128]
        lhs = jnp.concatenate([hi, hi, vlo[rows, t * CB : t * CB + CB], mix, mix], axis=1)
        return jnp.dot(lhs, w2[...], preferred_element_type=F32)

    def send_edges(r, tile, par, wait, start):
        if r == 0 or r == nb - 1:
            v = 0 if r == 0 else 1
            if wait:
                row_copy(v, par).wait_send()
                for h in range(2):
                    cor_copy(v, h, par).wait_send()
            for c0 in range(0, breadth, 128):
                x = tile(c0)
                rsend[v, :, c0 : c0 + 128] = x[:PAD] if v == 0 else x[RB - PAD :]
            if start:
                row_copy(v, par).start()
                for h in range(2):
                    cor_copy(v, h, par).start()
        for h in range(2):
            if wait:
                col_copy(h, r, par).wait_send()
            csend[h, r] = pack(tile(edge[h]), 0 if h == 0 else 96)
            if start:
                col_copy(h, r, par).start()

    def send_share(total, par):
        m = jnp.where(lane1 < 64, jnp.broadcast_to(total, (1, 128)), fsum[...])
        asend[...] = m
        arecv[par, j] = m
        for o in range(1, ngy):
            share_copy(o, par, j).start()

    def reduce_acc():
        return jnp.sum(jnp.sum(acc[...], axis=0, keepdims=True), axis=1, keepdims=True)

    def fold(c):
        return jnp.sum(c.reshape(RB // 8, 8, c.shape[1]), axis=0)

    def row_fog(par):
        for o in range(1, ngy):
            share_copy(o, par, lax.rem(j + o, ngy)).wait_recv()
        total = jnp.zeros((nj, 128), F32)
        before = gbuf[1]
        for s in range(ngy):
            w = jnp.where(lane1 < 64, 1.0, -before[s // per : s // per + 1, :])
            total = total + qc[s] * (arecv[par, s] * w)
        r = total + pltpu.roll(total, 64, 1)
        bsend[...] = r
        brecv[par, i] = r
        for o in range(1, ngx):
            fog_copy(o, par, i).start()

    def get_fog(par):
        for o in range(1, ngx):
            fog_copy(o, par, lax.rem(i + o, ngx)).wait_recv()
        for a in range(3):
            row = jnp.clip(i - 1 + a, 0, ni - 1)
            weight = pc[row]
            total = jnp.zeros((nj, 128), F32)
            for s in range(ngx):
                total = total + weight[s : s + 1, :] * brecv[par, s]
            gbuf[a] = total

    def fog_at(a, col):
        return gbuf[a, pl.ds(col, 1), :]

    def blur_first(par):
        for r in range(1, nb - 1):
            first_main(r)
        get_fog(1 - par)
        halo = []
        for v in range(2):
            row_wait(v, par)
            fog = fog_at(2 * v, blk_j)
            rows = slice(0, PAD) if v == 0 else slice(PAD + height, 2 * PAD + height)
            tiles = []
            for c0 in range(0, breadth, 128):
                x = rrecv[par, v, :, c0 : c0 + 128] - fog * frr[v, :, c0 : c0 + 128]
                x = jnp.where(has_x[v], x, 0.0)
                hi, lo = split(x)
                chi[rows, c0 : c0 + 128] = hi
                clo[rows, c0 : c0 + 128] = lo
                tiles.append(x)
            halo.append(tiles)
        for r in (0, nb - 1):
            first_main(r)
        for v in range(2):
            rows = slice(0, PAD) if v == 0 else slice(PAD + height, 2 * PAD + height)
            sides = []
            for h in range(2):
                cor_wait(v, h, par)
                x = krecv[par, v, h] - fog_at(2 * v, side_j[h]) * fkr[v, h]
                sides.append(roll(jnp.where(has_x[v] & has_y[h], x, 0.0), 32))
            put_side(rows, halo[v][1], halo[v][2], sides[0], sides[1], lane_pad)
        fogs = [fog_at(1, side_j[h]) for h in range(2)]
        for r in range(nb):
            rows = slice(r * RB, r * RB + RB)
            sides = []
            for h in range(2):
                col_wait(h, r, par)
                x = crecv[par, h, r] - fogs[h] * fcr[h, r]
                sides.append(unpack(jnp.where(has_y[h], x, 0.0), 32 * h))
            c1 = f[rows, 128:256] * d[rows, 128:256]
            c2 = f[rows, 256:384] * d[rows, 256:384]
            put_side(slice(PAD + r * RB, PAD + r * RB + RB), c1, c2, sides[0], sides[1], lane_rb)
        for r in range(nb):
            put_mix(r, first_dot(r, nt))

    def advance(k, carry):
        par = lax.rem(k, 2)
        nxt = 1 - par
        blur_first(par)
        own = wide(fog_at(1, blk_j))
        order = [0, nb - 1] + list(range(1, nb - 1))
        for n, r in enumerate(order):
            rows = slice(r * RB, r * RB + RB)
            c = []
            for t in range(nt):
                cs = slice(t * CB, t * CB + CB)
                back = second_dot(r, t)
                now = d[rows, cs] - own
                cov = f[rows, cs]
                new = (now + 0.75) - 0.75 * (cov * now) - back + own * u[rows, cs]
                d[rows, cs] = new
                x = cov * new
                hi, lo = split(x)
                chi[PAD + r * RB : PAD + r * RB + RB, cs] = hi
                clo[PAD + r * RB : PAD + r * RB + RB, cs] = lo
                acc[:, cs] = fold(x) if n == 0 else acc[:, cs] + fold(x)
                c.append(x)
            send_edges(r, lambda c0: c[c0 // CB][:, c0 % CB : c0 % CB + 128], nxt, True, True)
            if n == 1:
                for o in range(1, ngx):
                    fog_copy(o, par, i).wait_send()
                row_fog(par)
        for o in range(1, ngy):
            share_copy(o, par, j).wait_send()
        send_share(reduce_acc(), nxt)
        return carry

    loads = []
    for r in range(nb):
        rows = pl.ds(r * RB, RB)
        loads.append((pltpu.make_async_copy(cover_hbm.at[rows], cover.at[rows], in_sem.at[0, r]),
                      pltpu.make_async_copy(dose_hbm.at[rows], d.at[rows], in_sem.at[1, r])))
    order = [0, nb - 1] + list(range(1, nb - 1))
    for r in order:
        for c in loads[r]:
            c.start()
    consts = [pltpu.make_async_copy(s, t, in_sem.at[2, n])
              for n, (s, t) in enumerate(((a1_hbm, a1), (w2_hbm, w2), (qc_hbm, qc), (pc_hbm, pc)))]
    for c in consts:
        c.start()

    barrier = pltpu.get_barrier_semaphore()
    partners = [dev(i, lax.rem(j + o, ngy)) for o in range(1, ngy)]
    partners += [dev(lax.rem(i + o, ngx), j) for o in range(1, ngx)]
    partners += [dev(x, y) for x in step_x for y in step_y]
    for p in partners:
        pl.semaphore_signal(barrier, inc=1, device_id=p, device_id_type=MESH)

    bsend[...] = jnp.zeros_like(bsend)
    brecv[1, i] = jnp.zeros(bsend.shape, F32)
    chi[0:PAD, :] = jnp.zeros((PAD, chi.shape[1]), BF)
    chi[PAD + height :, :] = jnp.zeros((PAD, chi.shape[1]), BF)

    zero = jnp.zeros((RB, 128), F32)
    for n, r in enumerate(order):
        rows = slice(r * RB, r * RB + RB)
        for c in loads[r]:
            c.wait()
        for t in range(nt):
            cs = slice(t * CB, t * CB + CB)
            cov = cover[rows, cs].astype(F32) * (1.0 / 64.0)
            f[rows, cs] = cov
            x = cov * d[rows, cs]
            acc[:, cs] = fold(x) if n == 0 else acc[:, cs] + fold(x)
            chi[PAD + r * RB : PAD + r * RB + RB, cs] = cov.astype(BF)
        if n == 0:
            pl.semaphore_wait(barrier, len(partners))
        send_edges(r, lambda c0: f[rows, c0 : c0 + 128] * d[rows, c0 : c0 + 128], 0, False, True)
    share = reduce_acc()
    total = jnp.zeros((8, breadth), F32)
    for r in range(nb):
        rows = slice(r * RB, r * RB + RB)
        total = total + fold(f[rows, :])
        for h in range(2):
            fcs[h, r] = pack(f[rows, edge[h] : edge[h] + 128], 0 if h == 0 else 96)
    frs[0] = f[0:PAD, :]
    frs[1] = f[height - PAD :, :]
    fsum[...] = jnp.broadcast_to(
        jnp.sum(jnp.sum(total, axis=0, keepdims=True), axis=1, keepdims=True), (1, 128))
    send_share(share, 0)
    for o in range(1, ngx):
        fog_copy(o, 1, i).start()
    for v in range(2):
        frow_copy(v, 1 - v).start()
        fcol_copy(v, 1 - v).start()
        for h in range(2):
            fcor_copy(v, h, 1 - v, 1 - h).start()

    for c in consts:
        c.wait()
    for r in range(nb):
        rows = slice(PAD + r * RB, PAD + r * RB + RB)
        own_rows = slice(r * RB, r * RB + RB)
        for n, (c0, keep) in enumerate(((256, 1), (128, 0))):
            x = roll(f[own_rows, c0 : c0 + 128], 32)
            e = jnp.where((lane_rb < 32) if keep == 0 else (lane_rb >= 32), x, zero)
            e = jnp.where(lane_rb < 64, e, roll(e, 64))
            chi[rows, breadth + 128 * n : breadth + 128 * n + 128] = e.astype(BF)
    wide_first = 2 * (RB + 2 * PAD)
    for r in range(nb):
        rows = slice(r * RB, r * RB + RB + 2 * PAD)
        for n in range(nt + 1):
            cs = slice(n * CB, n * CB + CB)
            hi = chi[rows, cs]
            v = jnp.dot(a1[:, :wide_first], jnp.concatenate([hi, hi], axis=0), preferred_element_type=F32)
            if n == nt:
                put_mix(r, v)
            else:
                hi, lo = split(v)
                vhi[r * RB : r * RB + RB, cs] = hi
                vlo[r * RB : r * RB + RB, cs] = lo
    for r in range(nb):
        rows = slice(r * RB, r * RB + RB)
        for t in range(nt):
            cs = slice(t * CB, t * CB + CB)
            u[rows, cs] = second_dot(r, t)
    for r in range(nb):
        rows = slice(r * RB, r * RB + RB)
        for t in range(nt):
            cs = slice(t * CB, t * CB + CB)
            hi, lo = split(f[rows, cs] * d[rows, cs])
            chi[PAD + r * RB : PAD + r * RB + RB, cs] = hi
            clo[PAD + r * RB : PAD + r * RB + RB, cs] = lo

    for v in range(2):
        frow_copy(v, v).wait_recv()
        fcol_copy(v, v).wait_recv()
        for h in range(2):
            fcor_copy(v, h, v, h).wait_recv()

    lax.fori_loop(0, ITERS - 1, advance, 0)

    par = (ITERS - 1) % 2
    blur_first(par)
    own = wide(fog_at(1, blk_j))
    for o in range(1, ngx):
        fog_copy(o, par, i).wait_send()
    row_fog(par)
    get_fog(par)
    last = wide(fog_at(1, blk_j))
    stores = []
    for r in range(nb):
        rows = slice(r * RB, r * RB + RB)
        for t in range(nt):
            cs = slice(t * CB, t * CB + CB)
            back = second_dot(r, t)
            now = d[rows, cs] - own
            change = (0.75 - last) - 0.75 * (f[rows, cs] * now) - back + own * u[rows, cs]
            d[rows, cs] = now + change
            u[rows, cs] = change * (1.0 / 1.5)
        for n, (src, dst) in enumerate(((d, out_d), (u, out_r))):
            c = pltpu.make_async_copy(src.at[pl.ds(r * RB, RB)], dst.at[pl.ds(r * RB, RB)], out_sem.at[n, r])
            c.start()
            stores.append(c)
    for v in range(2):
        row_copy(v, par).wait_send()
        frow_copy(v, v).wait_send()
        fcol_copy(v, v).wait_send()
        for h in range(2):
            cor_copy(v, h, par).wait_send()
            fcor_copy(v, h, v, h).wait_send()
        for r in range(nb):
            col_copy(v, r, par).wait_send()
    for o in range(1, ngy):
        share_copy(o, par, j).wait_send()
    for o in range(1, ngx):
        fog_copy(o, par, i).wait_send()
    for c in stores:
        c.wait()


def per_device(ngx, ngy, coverage, dose):
    height, breadth = dose.shape
    nb = height // RB
    ni, nj = ngx * height // COARSE, ngy * breadth // COARSE
    per = COARSE // breadth
    spread_j = fog_matrix(nj) / float(COARSE * COARSE)
    qc = np.stack([np.broadcast_to(spread_j[:, s // per, None], (nj, 128)) for s in range(ngy)])
    pc = np.broadcast_to(0.225 * fog_matrix(ni)[:, :, None], (ni, ni, 128))
    dma = pltpu.SemaphoreType.DMA
    vm = pltpu.VMEM
    wide_cols = breadth + 256
    any_spec = pl.BlockSpec(memory_space=pl.ANY)
    tile = jax.ShapeDtypeStruct((height, breadth), F32)
    return pl.pallas_call(
        functools.partial(kernel, ngx, ngy),
        out_shape=(tile, tile),
        in_specs=[any_spec] * 6,
        out_specs=(any_spec, any_spec),
        scratch_shapes=[
            vm((height, breadth), jnp.int32), vm((height, breadth), F32), vm((height, breadth), F32),
            vm((height, breadth), F32),
            vm((RB, 3 * (RB + 2 * PAD)), BF), vm((4 * CB, CB), BF), vm(qc.shape, F32), vm(pc.shape, F32),
            vm((height + 2 * PAD, wide_cols), BF), vm((height + 2 * PAD, wide_cols), BF),
            vm((height, breadth), BF), vm((height, breadth), BF), vm((height, 256), BF),
            vm((8, breadth), F32), vm((3, nj, 128), F32), vm((1, 128), F32),
            vm((2, PAD, breadth), F32), vm((2, 2, PAD, breadth), F32),
            vm((2, nb, RB // 4, 128), F32), vm((2, 2, nb, RB // 4, 128), F32),
            vm((2, 2, 2, PAD, 128), F32),
            vm((2, PAD, breadth), F32), vm((2, PAD, breadth), F32),
            vm((2, nb, RB // 4, 128), F32), vm((2, nb, RB // 4, 128), F32),
            vm((2, 2, PAD, 128), F32),
            vm((1, 128), F32), vm((2, ngy, 1, 128), F32), vm((nj, 128), F32), vm((2, ngx, nj, 128), F32),
            dma((3, nb)), dma((2, nb)),
            dma((2,)), dma((2, 2)), dma((2, nb)), dma((2, 2, nb)), dma((2, 2)), dma((2, 2, 2)),
            dma((2,)), dma((2,)), dma((2,)), dma((2,)), dma((2, 2)), dma((2, 2)),
            dma((ngy,)), dma((2, ngy)), dma((ngx,)), dma((2, ngx)),
        ],
        compiler_params=pltpu.CompilerParams(
            collective_id=0, has_side_effects=True, vmem_limit_bytes=56 * 2**20
        ),
    )(coverage, dose, jnp.asarray(band_first()), jnp.asarray(band_second()),
      jnp.asarray(qc, F32), jnp.asarray(pc, F32))


def solution(mesh):
    return jax.shard_map(
        functools.partial(per_device, mesh.shape["gx"], mesh.shape["gy"]),
        mesh=mesh,
        in_specs=(P("gx", "gy"), P("gx", "gy")),
        out_specs=(P("gx", "gy"), P("gx", "gy")),
        check_vma=False,
    )
```

```python
import functools
import math

import jax
import jax.numpy as jnp
import numpy as np
from jax import lax
from jax.experimental import pallas as pl
from jax.experimental.pallas import tpu as pltpu
from jax.sharding import PartitionSpec as P

RIM = 30
PAD = 32
COARSE = 1024
FOG = 3072
ITERS = 6
RB = 256
CB = 256
KW = RB + 2 * PAD
BF = jnp.bfloat16
F32 = jnp.float32
MESH = pl.DeviceIdType.MESH


def two_terms(x):
    hi = np.asarray(x, np.float32).astype(BF)
    lo = (x - hi.astype(np.float64)).astype(np.float32).astype(BF)
    return hi, lo


def taps():
    k = np.arange(-RIM, RIM + 1).astype(np.float64)
    w = np.exp(-k * k / 200.0)
    return w / w.sum()


def band_first():
    w = taps()
    band = np.zeros((RB, KW))
    for i in range(RB):
        band[i, i + PAD - RIM : i + PAD + RIM + 1] = w
    hi, lo = two_terms(band)
    return np.concatenate([hi, lo, hi], axis=1)


def band_rows():
    w = taps()
    out = []
    for offset in (-PAD, PAD):
        band = np.array([[w[m + offset - i + RIM] if abs(m + offset - i) <= RIM else 0.0
                          for m in range(PAD)] for i in range(PAD)])
        hi, lo = two_terms(band)
        out.append(np.concatenate([hi, lo, hi, np.zeros_like(hi)], axis=1))
    return np.stack(out)


def second_weights(columns, outputs):
    w = 0.525 * taps()
    return np.array([[w[c - j + RIM] if abs(c - j) <= RIM else 0.0 for j in outputs] for c in columns])


def band_second():
    out = []
    for beside in (range(CB, CB + 128), range(-128, 0)):
        mh, ml = two_terms(second_weights(range(CB), range(CB)))
        xh, xl = two_terms(second_weights(beside, range(CB)))
        out.append(np.concatenate([mh, ml, mh, xh, xl, xh], axis=0))
    return np.stack(out)


def band_halo(breadth):
    columns = list(range(-PAD, 0)) + list(range(breadth, breadth + PAD))
    outputs = list(range(128)) + list(range(breadth - 128, breadth))
    hi, lo = two_terms(second_weights(columns, outputs))
    return np.concatenate([hi, hi, lo, lo], axis=0)


def fog_matrix(n):
    s = FOG / COARSE
    k = np.arange(n).astype(np.float64)
    spread = k[:, None] - k[None, :]
    return np.exp(-spread * spread / (2.0 * s * s)) / (math.sqrt(2.0 * math.pi) * s)


def split(x):
    hi = x.astype(BF)
    return hi, (x - hi.astype(F32)).astype(BF)


def wide(row, n):
    return jnp.concatenate([row] * n, axis=1)


def kernel(ngx, ngy, cover_hbm, dose_hbm, a1_hbm, w2_hbm, wh_hbm, ah_hbm, qc_hbm, pc_hbm, d, out_r,
           cover, f, w, a1, w2, wh, ah, qc, pc, chi, clo, whi, wlo, we, acc, gbuf, fsum, uh,
           rsend, rrecv, csend, crecv, ksend, krecv, frr, fcs, fcr, fks, fkr, fce, fke,
           asend, arecv, bsend, brecv,
           in_sem, row_s, row_r, col_s, col_r, cor_s, cor_r,
           frow_s, frow_r, fcol_s, fcol_r, fcor_s, fcor_r, fa_s, fa_r, fb_s, fb_r):
    height, breadth = d.shape
    nb = height // RB
    nt = breadth // CB
    per = COARSE // breadth
    ni, nj = ngx * height // COARSE, ngy * breadth // COARSE
    i, j = lax.axis_index("gx"), lax.axis_index("gy")
    step_x = (lax.rem(i + ngx - 1, ngx), lax.rem(i + 1, ngx))
    has_x = (i > 0, i < ngx - 1)
    has_y = (j > 0, j < ngy - 1)
    step_y = (jnp.maximum(j - 1, 0), jnp.minimum(j + 1, ngy - 1))
    beside = tuple(jnp.where(has_y[h], i, i + 1 - 2 * lax.rem(i, 2)) for h in range(2))
    into = tuple(jnp.where(has_y[h], 1 - h, h) for h in range(2))
    blk_j = j // per
    side_j = (step_y[0] // per, step_y[1] // per)
    edge = (0, breadth - 128)
    center = slice(128, breadth - 128)
    left, right = slice(0, 128), slice(breadth - 128, breadth)

    def dev(x, y):
        return {"gx": x, "gy": y}

    def remote(src, dst, ss, rs, to):
        return pltpu.make_async_remote_copy(
            src_ref=src, dst_ref=dst, send_sem=ss, recv_sem=rs, device_id=to, device_id_type=MESH
        )

    def row_copy(v, par, slot):
        return remote(rsend.at[v], rrecv.at[par, slot], row_s.at[v], row_r.at[par, slot], dev(step_x[v], j))

    def col_copy(h, r, par, slot):
        return remote(csend.at[h, r], crecv.at[par, slot, r], col_s.at[h, r], col_r.at[par, slot, r],
                      dev(beside[h], step_y[h]))

    def cor_copy(v, h, par, sv, sh):
        return remote(ksend.at[v, h], krecv.at[par, sv, sh], cor_s.at[v, h], cor_r.at[par, sv, sh],
                      dev(step_x[v], step_y[h]))

    def frow_copy(v, slot):
        return remote(f.at[pl.ds(v * (height - PAD), PAD)], frr.at[slot], frow_s.at[v], frow_r.at[slot],
                      dev(step_x[v], j))

    def fcol_copy(h, slot):
        return remote(fcs.at[h], fcr.at[slot], fcol_s.at[h], fcol_r.at[slot], dev(beside[h], step_y[h]))

    def fcor_copy(v, h, sv, sh):
        return remote(fks.at[v, h], fkr.at[sv, sh], fcor_s.at[v, h], fcor_r.at[sv, sh],
                      dev(step_x[v], step_y[h]))

    def share_copy(o, par, slot):
        return remote(asend, arecv.at[par, slot], fa_s.at[o], fa_r.at[par, slot],
                      dev(i, lax.rem(j + o, ngy)))

    def fog_copy(o, par, slot):
        return remote(bsend, brecv.at[par, slot], fb_s.at[o], fb_r.at[par, slot],
                      dev(lax.rem(i + o, ngx), j))

    lane1 = lax.broadcasted_iota(jnp.int32, (1, 128), 1)

    def lanes(n):
        return lax.broadcasted_iota(jnp.int32, (n, 128), 1)

    def roll(x, shift):
        shift = shift % 128
        return x if shift == 0 else pltpu.roll(x, shift, 1)

    def pack(tile, first_lane):
        n = tile.shape[0] // 4
        lane = lanes(n)
        parts = [roll(tile[n * q : n * q + n], 32 * q - first_lane) for q in range(4)]
        low = jnp.where(lane < 32, parts[0], parts[1])
        high = jnp.where(lane < 96, parts[2], parts[3])
        return jnp.where(lane < 64, low, high)

    def unpack(piece, first_lane):
        return jnp.concatenate([roll(piece, first_lane - 32 * q) for q in range(4)], axis=0)

    def mix_ends(low, high):
        lane = lanes(low.shape[0])
        e = jnp.where(lane < 32, low, high)
        e = jnp.where(lane < 64, e, roll(e, 64))
        hi = e.astype(BF).astype(F32)
        return jnp.where(lane < 64, hi, e - hi).astype(BF)

    def put_charge(r, cs, x):
        hi, lo = split(x)
        chi[PAD + r * RB : PAD + r * RB + RB, cs] = hi
        clo[PAD + r * RB : PAD + r * RB + RB, cs] = lo

    def put_blur(rows, cs, x):
        hi, lo = split(x)
        whi[rows, cs] = hi
        wlo[rows, cs] = lo

    def put_main(rows, t, x):
        if t == 0:
            we[rows, 0:128] = x[:, :128]
            put_blur(rows, slice(128, CB), x[:, 128:])
        else:
            put_blur(rows, slice(CB, breadth - 128), x[:, :128])
            we[rows, 128:256] = x[:, 128:]

    def first_dot(r, pick):
        rows = slice(r * RB, r * RB + KW)
        hi = pick(whi, rows)
        return jnp.dot(a1[...], jnp.concatenate([hi, hi, pick(wlo, rows)], axis=0),
                       preferred_element_type=F32)

    def pick_center(ref, rows):
        return ref[rows, center]

    def pick_ends(ref, rows):
        return jnp.concatenate([ref[rows, left], ref[rows, right]], axis=1)

    def second_dot(hi, lo, t):
        own = slice(t * CB, t * CB + CB)
        other = slice(CB, CB + 128) if t == 0 else slice(CB - 128, CB)
        lhs = jnp.concatenate(
            [hi[:, own], hi[:, own], lo[:, own], hi[:, other], hi[:, other], lo[:, other]], axis=1)
        return jnp.dot(lhs, w2[t], preferred_element_type=F32)

    def block_rows(r):
        return slice(PAD + r * RB, PAD + r * RB + RB)

    def fold(x):
        return jnp.sum(x.reshape(x.shape[0] // 8, 8, x.shape[1]), axis=0)

    def add_acc(r, cs, x):
        acc[:, cs] = fold(x) if r == 0 else acc[:, cs] + fold(x)

    def reduce_acc():
        return jnp.sum(jnp.sum(acc[...], axis=0, keepdims=True), axis=1, keepdims=True)

    def fill_edges(r, sides, mids):
        for h in range(2):
            csend[h, r] = pack(sides[h], 96 * h)
        if r == 0 or r == nb - 1:
            v = 0 if r == 0 else 1
            part = slice(0, PAD) if v == 0 else slice(RB - PAD, RB)
            rsend[v, :, left] = sides[0][part]
            rsend[v, :, right] = sides[1][part]
            rsend[v, :, center] = mids[part]
            for h in range(2):
                ksend[v, h] = pack(sides[h][part], 96 * h)

    def start_edges(r, par):
        for h in range(2):
            col_copy(h, r, par, into[h]).start()
        if r == 0 or r == nb - 1:
            v = 0 if r == 0 else 1
            row_copy(v, par, 1 - v).start()
            for h in range(2):
                cor_copy(v, h, par, 1 - v, into[h]).start()

    def sent_edges(r):
        for h in range(2):
            col_copy(h, r, 0, h).wait_send()
        if r == 0 or r == nb - 1:
            v = 0 if r == 0 else 1
            row_copy(v, 0, v).wait_send()
            for h in range(2):
                cor_copy(v, h, 0, v, h).wait_send()

    def send_share(total, par):
        m = jnp.where(lane1 < 64, jnp.broadcast_to(total, (1, 128)), fsum[...])
        asend[...] = m
        arecv[par, j] = m
        for o in range(1, ngy):
            share_copy(o, par, j).start()

    def row_fog(par):
        for o in range(1, ngy):
            share_copy(o, par, lax.rem(j + o, ngy)).wait_recv()
        total = jnp.zeros((nj, 128), F32)
        before = gbuf[1]
        for s in range(ngy):
            m = jnp.where(lane1 < 64, 1.0, -before[s // per : s // per + 1, :])
            total = total + qc[s] * (arecv[par, s] * m)
        r = total + pltpu.roll(total, 64, 1)
        bsend[...] = r
        brecv[par, i] = r
        for o in range(1, ngx):
            fog_copy(o, par, i).start()

    def get_fog(par):
        for o in range(1, ngx):
            fog_copy(o, par, lax.rem(i + o, ngx)).wait_recv()
        for a in range(3):
            row = jnp.clip(i - 1 + a, 0, ni - 1)
            weight = pc[row]
            total = jnp.zeros((nj, 128), F32)
            for s in range(ngx):
                total = total + weight[s : s + 1, :] * brecv[par, s]
            gbuf[a] = total

    def fog_at(a, col):
        return gbuf[a, pl.ds(col, 1), :]

    def blur_inner(par, last):
        def block(r):
            rows = slice(r * RB, r * RB + RB)
            now = d[rows, center]
            change = 0.75 - 0.75 * (f[rows, center] * now) - first_dot(r, pick_center)
            if last:
                out_r[rows, center] = change
            else:
                d[rows, center] = now + change

        for r in range(nb):
            rows = block_rows(r)
            for t in range(nt):
                put_main(rows, t, second_dot(chi[rows, :], clo[rows, :], t))
        for r in range(1, nb - 1):
            block(r)
        halo = []
        for v in range(2):
            row_copy(v, par, v).wait_recv()
        for v in range(2):
            halo.append(split(jnp.where(has_x[v], rrecv[par, v], 0.0)))
        hi = jnp.concatenate([halo[0][0], halo[1][0]], axis=0)
        lo = jnp.concatenate([halo[0][1], halo[1][1]], axis=0)
        for t in range(nt):
            x = second_dot(hi, lo, t)
            put_main(slice(0, PAD), t, x[:PAD])
            put_main(slice(PAD + height, 2 * PAD + height), t, x[PAD:])
        for r in (0, nb - 1):
            block(r)

    def fog_rows(r, x, cs):
        n = (cs.stop - cs.start) // 128
        if r == 0:
            first = x[:PAD] + wide(fog_at(0, blk_j), n) * uh[0, :, cs]
            return jnp.concatenate([first, x[PAD:]], axis=0)
        if r == nb - 1:
            final = x[RB - PAD :] + wide(fog_at(2, blk_j), n) * uh[1, :, cs]
            return jnp.concatenate([x[: RB - PAD], final], axis=0)
        return x

    def get_corners(v, par):
        sides = []
        for h in range(2):
            x = krecv[par, v, h] - fog_at(2 * v, side_j[h]) * fke[v, h]
            sides.append(unpack(jnp.where(has_x[v] & has_y[h], x, 0.0), 32 * h))
        return mix_ends(sides[0], sides[1])

    def get_columns(r, par):
        sides = []
        for h in range(2):
            x = crecv[par, h, r] - fog_at(1, side_j[h]) * fce[h, r]
            sides.append(unpack(jnp.where(has_y[h], x, 0.0), 32 * h))
        return mix_ends(sides[0], sides[1])

    def put_ends(first, mix):
        rows = slice(first, first + mix.shape[0])
        x = we[rows, :] + jnp.dot(jnp.concatenate([mix, mix], axis=1), wh[...], preferred_element_type=F32)
        put_blur(rows, left, x[:, :128])
        put_blur(rows, right, x[:, 128:])

    def blur_ends(par, use):
        half = nb // 2
        for h in range(2):
            cor_copy(0, h, par, 0, h).wait_recv()
            for r in range(half + 1):
                col_copy(h, r, par, h).wait_recv()
        for r in range(nb):
            sent_edges(r)
        put_ends(0, jnp.concatenate(
            [get_corners(0, par)] + [get_columns(r, par) for r in range(half + 1)], axis=0))
        use([(r, first_dot(r, pick_ends)) for r in range(half)])
        for h in range(2):
            cor_copy(1, h, par, 1, h).wait_recv()
            for r in range(half + 1, nb):
                col_copy(h, r, par, h).wait_recv()
        put_ends(PAD + (half + 1) * RB, jnp.concatenate(
            [get_columns(r, par) for r in range(half + 1, nb)] + [get_corners(1, par)], axis=0))
        use([(r, first_dot(r, pick_ends)) for r in range(half, nb)])

    def advance(k, carry):
        par = lax.rem(k, 2)
        nxt = 1 - par
        blur_inner(par, False)
        get_fog(1 - par)

        @pl.when(k == 1)
        def _():
            own_halo_coverage()

        own = fog_at(1, blk_j)
        for r in range(nb):
            rows = slice(r * RB, r * RB + RB)
            new = d[rows, center] + wide(own, (breadth - 256) // 128) * w[rows, center]
            new = fog_rows(r, new, center)
            d[rows, center] = new
            x = f[rows, center] * new
            put_charge(r, center, x)
            add_acc(r, center, x)

        def use(backs):
            for r, back in backs:
                rows = slice(r * RB, r * RB + RB)
                sides = []
                for h in range(2):
                    cs = slice(edge[h], edge[h] + 128)
                    now = d[rows, cs]
                    cov = f[rows, cs]
                    new = now + (0.75 - 0.75 * (cov * now) - back[:, 128 * h : 128 * h + 128])
                    new = fog_rows(r, new + own * w[rows, cs], cs)
                    d[rows, cs] = new
                    x = cov * new
                    put_charge(r, cs, x)
                    add_acc(r, cs, x)
                    sides.append(x)
                fill_edges(r, sides, f[rows, center] * d[rows, center])
            for r, _ in backs:
                start_edges(r, nxt)

        blur_ends(par, use)
        for o in range(1, ngx):
            fog_copy(o, par, i).wait_send()
        row_fog(par)
        for o in range(1, ngy):
            share_copy(o, par, j).wait_send()
        send_share(reduce_acc(), nxt)
        return carry

    def own_halo_coverage():
        for v in range(2):
            frow_copy(v, v).wait_recv()
            fcol_copy(v, v).wait_recv()
            for h in range(2):
                fcor_copy(v, h, v, h).wait_recv()
        fce[...] = fcr[...]
        fke[...] = fkr[...]
        halo = jnp.concatenate([jnp.where(has_x[v], frr[v], 0.0) for v in range(2)], axis=0).astype(BF)
        for t in range(nt):
            hi, lo = split(second_dot(halo, jnp.zeros_like(halo), t))
            for v in range(2):
                part = slice(v * PAD, v * PAD + PAD)
                terms = jnp.concatenate([hi[part], hi[part], lo[part], jnp.zeros((PAD, CB), BF)], axis=0)
                uh[v, :, t * CB : t * CB + CB] = jnp.dot(ah[v], terms, preferred_element_type=F32)

    loads = []
    for r in range(nb):
        rows = pl.ds(r * RB, RB)
        loads.append((pltpu.make_async_copy(cover_hbm.at[rows], cover.at[rows], in_sem.at[0, r]),
                      pltpu.make_async_copy(dose_hbm.at[rows], d.at[rows], in_sem.at[1, r])))
        for c in loads[r]:
            c.start()
    pairs = ((a1_hbm, a1), (w2_hbm, w2), (wh_hbm, wh), (ah_hbm, ah), (qc_hbm, qc), (pc_hbm, pc))
    consts = [pltpu.make_async_copy(s, t, in_sem.at[2, n]) for n, (s, t) in enumerate(pairs)]
    for c in consts:
        c.start()

    barrier = pltpu.get_barrier_semaphore()
    partners = [dev(step_x[v], step_y[h]) for v in range(2) for h in range(2)]
    partners += [dev(i, lax.rem(j + o, ngy)) for o in range(1, ngy)]
    partners += [dev(lax.rem(i + o, ngx), j) for o in range(1, ngx)]
    for p in partners:
        pl.semaphore_signal(barrier, inc=1, device_id=p, device_id_type=MESH)

    bsend[...] = jnp.zeros_like(bsend)
    brecv[1, i] = jnp.zeros(bsend.shape, F32)
    uh[...] = jnp.zeros_like(uh)
    fce[...] = jnp.zeros_like(fce)
    fke[...] = jnp.zeros_like(fke)
    clo[...] = jnp.zeros_like(clo)
    for ref in (whi, wlo):
        ref[0:PAD, :] = jnp.zeros((PAD, breadth), BF)
        ref[PAD + height :, :] = jnp.zeros((PAD, breadth), BF)

    total = jnp.zeros((8, breadth), F32)
    for r in range(nb):
        rows = slice(r * RB, r * RB + RB)
        for c in loads[r]:
            c.wait()
        cov = cover[rows, :].astype(F32) * (1.0 / 64.0)
        f[rows, :] = cov
        total = total + fold(cov)
        chi[PAD + r * RB : PAD + r * RB + RB, :] = cov.astype(BF)
        for h in range(2):
            fcs[h, r] = pack(cov[:, edge[h] : edge[h] + 128], 96 * h)
            if r == 0:
                fks[0, h] = pack(cov[:PAD, edge[h] : edge[h] + 128], 96 * h)
            if r == nb - 1:
                fks[1, h] = pack(cov[RB - PAD :, edge[h] : edge[h] + 128], 96 * h)
        x = cov * d[rows, :]
        add_acc(r, slice(0, breadth), x)
        fill_edges(r, (x[:, left], x[:, right]), x[:, center])
    fsum[...] = jnp.broadcast_to(
        jnp.sum(jnp.sum(total, axis=0, keepdims=True), axis=1, keepdims=True), (1, 128))
    share = reduce_acc()

    for c in consts:
        c.wait()
    for r in range(nb):
        rows = block_rows(r)
        for t in range(nt):
            put_blur(rows, slice(t * CB, t * CB + CB), second_dot(chi[rows, :], clo[rows, :], t))
    for r in range(nb):
        rows = slice(r * RB, r * RB + RB)
        for t in range(nt):
            cs = slice(t * CB, t * CB + CB)
            u = first_dot(r, lambda ref, win: ref[win, cs])
            w[rows, cs] = u + 0.75 * f[rows, cs] - 1.0

    pl.semaphore_wait(barrier, len(partners))
    for r in range(nb):
        start_edges(r, 0)
    send_share(share, 0)
    for o in range(1, ngx):
        fog_copy(o, 1, i).start()
    for v in range(2):
        frow_copy(v, 1 - v).start()
        fcol_copy(v, into[v]).start()
        for h in range(2):
            fcor_copy(v, h, 1 - v, into[h]).start()
    for r in range(nb):
        rows = slice(r * RB, r * RB + RB)
        put_charge(r, slice(0, breadth), f[rows, :] * d[rows, :])

    lax.fori_loop(0, ITERS - 1, advance, 0)

    par = (ITERS - 1) % 2
    blur_inner(par, True)
    get_fog(1 - par)
    own = fog_at(1, blk_j)
    for r in range(nb):
        rows = slice(r * RB, r * RB + RB)
        now = d[rows, center] - wide(own, (breadth - 256) // 128)
        change = out_r[rows, center] + wide(own, (breadth - 256) // 128) * (w[rows, center] + 1.0)
        change = fog_rows(r, change, center)
        d[rows, center] = now
        out_r[rows, center] = change

    def use_last(backs):
        for r, back in backs:
            rows = slice(r * RB, r * RB + RB)
            for h in range(2):
                cs = slice(edge[h], edge[h] + 128)
                now = d[rows, cs]
                change = 0.75 - 0.75 * (f[rows, cs] * now) - back[:, 128 * h : 128 * h + 128]
                change = change + own * (w[rows, cs] + 1.0)
                d[rows, cs] = now - own
                out_r[rows, cs] = fog_rows(r, change, cs)

    blur_ends(par, use_last)
    for o in range(1, ngx):
        fog_copy(o, par, i).wait_send()
    row_fog(par)
    get_fog(par)
    last = wide(fog_at(1, blk_j), breadth // 128)
    for r in range(nb):
        rows = slice(r * RB, r * RB + RB)
        change = out_r[rows, :] - last
        d[rows, :] = d[rows, :] + change
        out_r[rows, :] = change * (1.0 / 1.5)
    for v in range(2):
        frow_copy(v, v).wait_send()
        fcol_copy(v, v).wait_send()
        for h in range(2):
            fcor_copy(v, h, v, h).wait_send()
    for o in range(1, ngy):
        share_copy(o, par, j).wait_send()
    for o in range(1, ngx):
        fog_copy(o, par, i).wait_send()


def per_device(ngx, ngy, coverage, dose):
    height, breadth = dose.shape
    nb = height // RB
    ni, nj = ngx * height // COARSE, ngy * breadth // COARSE
    per = COARSE // breadth
    spread_j = fog_matrix(nj) / float(COARSE * COARSE)
    qc = np.stack([np.broadcast_to(spread_j[:, s // per, None], (nj, 128)) for s in range(ngy)])
    pc = np.broadcast_to(0.225 * fog_matrix(ni)[:, :, None], (ni, ni, 128))
    a1, w2, wh, ah = band_first(), band_second(), band_halo(breadth), band_rows()
    dma = pltpu.SemaphoreType.DMA
    vm = pltpu.VMEM
    any_spec = pl.BlockSpec(memory_space=pl.ANY)
    tile, padded = (height, breadth), (height + 2 * PAD, breadth)
    rows, cols, corners = (2, PAD, breadth), (2, nb, RB // 4, 128), (2, 2, PAD // 4, 128)
    return pl.pallas_call(
        functools.partial(kernel, ngx, ngy),
        out_shape=(vm(tile, F32), vm(tile, F32)),
        in_specs=[any_spec] * 8,
        out_specs=(pl.BlockSpec(memory_space=vm), pl.BlockSpec(memory_space=vm)),
        scratch_shapes=[
            vm(tile, jnp.int32), vm(tile, F32), vm(tile, F32),
            vm(a1.shape, BF), vm(w2.shape, BF), vm(wh.shape, BF), vm(ah.shape, BF), vm(qc.shape, F32), vm(pc.shape, F32),
            vm(padded, BF), vm(padded, BF), vm(padded, BF), vm(padded, BF), vm((height + 2 * PAD, 256), F32),
            vm((8, breadth), F32), vm((3, nj, 128), F32), vm((1, 128), F32), vm(rows, F32),
            vm(rows, F32), vm((2,) + rows, F32), vm(cols, F32), vm((2,) + cols, F32),
            vm(corners, F32), vm((2,) + corners, F32),
            vm(rows, F32), vm(cols, F32), vm(cols, F32), vm(corners, F32), vm(corners, F32),
            vm(cols, F32), vm(corners, F32),
            vm((1, 128), F32), vm((2, ngy, 1, 128), F32), vm((nj, 128), F32), vm((2, ngx, nj, 128), F32),
            dma((3, max(nb, 6))),
            dma((2,)), dma((2, 2)), dma((2, nb)), dma((2, 2, nb)), dma((2, 2)), dma((2, 2, 2)),
            dma((2,)), dma((2,)), dma((2,)), dma((2,)), dma((2, 2)), dma((2, 2)),
            dma((ngy,)), dma((2, ngy)), dma((ngx,)), dma((2, ngx)),
        ],
        compiler_params=pltpu.CompilerParams(
            collective_id=0, has_side_effects=True, vmem_limit_bytes=40 * 2**20
        ),
    )(coverage, dose, jnp.asarray(a1), jnp.asarray(w2), jnp.asarray(wh), jnp.asarray(ah),
      jnp.asarray(qc, F32), jnp.asarray(pc, F32))


def solution(mesh):
    return jax.shard_map(
        functools.partial(per_device, mesh.shape["gx"], mesh.shape["gy"]),
        mesh=mesh,
        in_specs=(P("gx", "gy"), P("gx", "gy")),
        out_specs=(P("gx", "gy"), P("gx", "gy")),
        check_vma=False,
    )
```

```python
import functools
import math

import jax
import jax.numpy as jnp
import numpy as np
from jax import lax
from jax.experimental import pallas as pl
from jax.experimental.pallas import tpu as pltpu
from jax.sharding import PartitionSpec as P

RIM = 30
PAD = 32
COARSE = 1024
FOG = 3072
ITERS = 6
RB = 256
CB = 256
KW = RB + 2 * PAD
BF = jnp.bfloat16
F32 = jnp.float32
MESH = pl.DeviceIdType.MESH


def two_terms(x):
    hi = np.asarray(x, np.float32).astype(BF)
    lo = (x - hi.astype(np.float64)).astype(np.float32).astype(BF)
    return hi, lo


def taps():
    k = np.arange(-RIM, RIM + 1).astype(np.float64)
    w = np.exp(-k * k / 200.0)
    return w / w.sum()


def band_first():
    w = taps()
    band = np.zeros((RB, KW))
    for i in range(RB):
        band[i, i + PAD - RIM : i + PAD + RIM + 1] = w
    hi, lo = two_terms(band)
    return np.concatenate([hi, lo, hi], axis=1)


def band_rows():
    w = taps()
    out = []
    for offset in (-PAD, PAD):
        band = np.array([[w[m + offset - i + RIM] if abs(m + offset - i) <= RIM else 0.0
                          for m in range(PAD)] for i in range(PAD)])
        hi, lo = two_terms(band)
        out.append(np.concatenate([hi, lo, hi, np.zeros_like(hi)], axis=1))
    return np.stack(out)


def second_weights(columns, outputs):
    w = 0.525 * taps()
    return np.array([[w[c - j + RIM] if abs(c - j) <= RIM else 0.0 for j in outputs] for c in columns])


def band_second():
    out = []
    for beside in (range(CB, CB + 128), range(-128, 0)):
        mh, ml = two_terms(second_weights(range(CB), range(CB)))
        xh, xl = two_terms(second_weights(beside, range(CB)))
        out.append(np.concatenate([mh, ml, mh, xh, xl, xh], axis=0))
    return np.stack(out)


def band_halo(breadth):
    columns = list(range(-PAD, 0)) + list(range(breadth, breadth + PAD))
    outputs = list(range(128)) + list(range(breadth - 128, breadth))
    hi, lo = two_terms(second_weights(columns, outputs))
    return np.concatenate([hi, hi, lo, lo], axis=0)


def fog_matrix(n):
    s = FOG / COARSE
    k = np.arange(n).astype(np.float64)
    spread = k[:, None] - k[None, :]
    return np.exp(-spread * spread / (2.0 * s * s)) / (math.sqrt(2.0 * math.pi) * s)


def split(x):
    hi = x.astype(BF)
    return hi, (x - hi.astype(F32)).astype(BF)


def wide(row, n):
    return jnp.concatenate([row] * n, axis=1)


def kernel(ngx, ngy, cover_hbm, dose_hbm, a1_hbm, w2_hbm, wh_hbm, ah_hbm, qc_hbm, pc_hbm, d, out_r,
           cover, f, w, a1, w2, wh, ah, qc, pc, chi, clo, whi, wlo, we, acc, gbuf, fsum, uh,
           rsend, rrecv, csend, crecv, ksend, krecv, frr, fcs, fcr, fks, fkr, fce, fke,
           asend, arecv, bsend, brecv,
           in_sem, row_s, row_r, col_s, col_r, cor_s, cor_r,
           frow_s, frow_r, fcol_s, fcol_r, fcor_s, fcor_r, fa_s, fa_r, fb_s, fb_r):
    height, breadth = d.shape
    nb = height // RB
    nt = breadth // CB
    per = COARSE // breadth
    ni, nj = ngx * height // COARSE, ngy * breadth // COARSE
    i, j = lax.axis_index("gx"), lax.axis_index("gy")
    step_x = (lax.rem(i + ngx - 1, ngx), lax.rem(i + 1, ngx))
    has_x = (i > 0, i < ngx - 1)
    has_y = (j > 0, j < ngy - 1)
    step_y = (jnp.maximum(j - 1, 0), jnp.minimum(j + 1, ngy - 1))
    beside = tuple(jnp.where(has_y[h], i, i + 1 - 2 * lax.rem(i, 2)) for h in range(2))
    into = tuple(jnp.where(has_y[h], 1 - h, h) for h in range(2))
    blk_j = j // per
    side_j = (step_y[0] // per, step_y[1] // per)
    edge = (0, breadth - 128)
    center = slice(128, breadth - 128)
    left, right = slice(0, 128), slice(breadth - 128, breadth)

    def dev(x, y):
        return {"gx": x, "gy": y}

    def remote(src, dst, ss, rs, to):
        return pltpu.make_async_remote_copy(
            src_ref=src, dst_ref=dst, send_sem=ss, recv_sem=rs, device_id=to, device_id_type=MESH
        )

    def row_copy(v, par, slot):
        return remote(rsend.at[v], rrecv.at[par, slot], row_s.at[v], row_r.at[par, slot], dev(step_x[v], j))

    def col_copy(h, r, par, slot):
        return remote(csend.at[h, r], crecv.at[par, slot, r], col_s.at[h, r], col_r.at[par, slot, r],
                      dev(beside[h], step_y[h]))

    def cor_copy(v, h, par, sv, sh):
        return remote(ksend.at[v, h], krecv.at[par, sv, sh], cor_s.at[v, h], cor_r.at[par, sv, sh],
                      dev(step_x[v], step_y[h]))

    def frow_copy(v, slot):
        return remote(f.at[pl.ds(v * (height - PAD), PAD)], frr.at[slot], frow_s.at[v], frow_r.at[slot],
                      dev(step_x[v], j))

    def fcol_copy(h, slot):
        return remote(fcs.at[h], fcr.at[slot], fcol_s.at[h], fcol_r.at[slot], dev(beside[h], step_y[h]))

    def fcor_copy(v, h, sv, sh):
        return remote(fks.at[v, h], fkr.at[sv, sh], fcor_s.at[v, h], fcor_r.at[sv, sh],
                      dev(step_x[v], step_y[h]))

    def share_copy(o, par, slot):
        return remote(asend, arecv.at[par, slot], fa_s.at[o], fa_r.at[par, slot],
                      dev(i, lax.rem(j + o, ngy)))

    def fog_copy(o, par, slot):
        return remote(bsend, brecv.at[par, slot], fb_s.at[o], fb_r.at[par, slot],
                      dev(lax.rem(i + o, ngx), j))

    lane1 = lax.broadcasted_iota(jnp.int32, (1, 128), 1)

    def lanes(n):
        return lax.broadcasted_iota(jnp.int32, (n, 128), 1)

    def roll(x, shift):
        shift = shift % 128
        return x if shift == 0 else pltpu.roll(x, shift, 1)

    def pack(tile, first_lane):
        n = tile.shape[0] // 4
        lane = lanes(n)
        parts = [roll(tile[n * q : n * q + n], 32 * q - first_lane) for q in range(4)]
        low = jnp.where(lane < 32, parts[0], parts[1])
        high = jnp.where(lane < 96, parts[2], parts[3])
        return jnp.where(lane < 64, low, high)

    def unpack(piece, first_lane):
        return jnp.concatenate([roll(piece, first_lane - 32 * q) for q in range(4)], axis=0)

    def mix_ends(low, high):
        lane = lanes(low.shape[0])
        e = jnp.where(lane < 32, low, high)
        e = jnp.where(lane < 64, e, roll(e, 64))
        hi = e.astype(BF).astype(F32)
        return jnp.where(lane < 64, hi, e - hi).astype(BF)

    def put_charge(r, cs, x):
        hi, lo = split(x)
        chi[PAD + r * RB : PAD + r * RB + RB, cs] = hi
        clo[PAD + r * RB : PAD + r * RB + RB, cs] = lo

    def put_blur(rows, cs, x):
        hi, lo = split(x)
        whi[rows, cs] = hi
        wlo[rows, cs] = lo

    def put_main(rows, t, x):
        if t == 0:
            we[rows, 0:128] = x[:, :128]
            put_blur(rows, slice(128, CB), x[:, 128:])
        else:
            put_blur(rows, slice(CB, breadth - 128), x[:, :128])
            we[rows, 128:256] = x[:, 128:]

    def first_dot(r, pick):
        rows = slice(r * RB, r * RB + KW)
        hi = pick(whi, rows)
        return jnp.dot(a1[...], jnp.concatenate([hi, hi, pick(wlo, rows)], axis=0),
                       preferred_element_type=F32)

    def pick_center(ref, rows):
        return ref[rows, center]

    def pick_ends(ref, rows):
        return jnp.concatenate([ref[rows, left], ref[rows, right]], axis=1)

    def second_dot(hi, lo, t):
        own = slice(t * CB, t * CB + CB)
        other = slice(CB, CB + 128) if t == 0 else slice(CB - 128, CB)
        lhs = jnp.concatenate(
            [hi[:, own], hi[:, own], lo[:, own], hi[:, other], hi[:, other], lo[:, other]], axis=1)
        return jnp.dot(lhs, w2[t], preferred_element_type=F32)

    def block_rows(r):
        return slice(PAD + r * RB, PAD + r * RB + RB)

    def fold(x):
        return jnp.sum(x.reshape(x.shape[0] // 8, 8, x.shape[1]), axis=0)

    def add_acc(r, cs, x):
        acc[:, cs] = fold(x) if r == 0 else acc[:, cs] + fold(x)

    def reduce_acc():
        return jnp.sum(jnp.sum(acc[...], axis=0, keepdims=True), axis=1, keepdims=True)

    def fill_edges(r, sides, mids):
        for h in range(2):
            csend[h, r] = pack(sides[h], 96 * h)
        if r == 0 or r == nb - 1:
            v = 0 if r == 0 else 1
            part = slice(0, PAD) if v == 0 else slice(RB - PAD, RB)
            rsend[v, :, left] = sides[0][part]
            rsend[v, :, right] = sides[1][part]
            rsend[v, :, center] = mids[part]
            for h in range(2):
                ksend[v, h] = pack(sides[h][part], 96 * h)

    def start_edges(r, par):
        for h in range(2):
            col_copy(h, r, par, into[h]).start()
        if r == 0 or r == nb - 1:
            v = 0 if r == 0 else 1
            row_copy(v, par, 1 - v).start()
            for h in range(2):
                cor_copy(v, h, par, 1 - v, into[h]).start()

    def sent_edges(r):
        for h in range(2):
            col_copy(h, r, 0, h).wait_send()
        if r == 0 or r == nb - 1:
            v = 0 if r == 0 else 1
            row_copy(v, 0, v).wait_send()
            for h in range(2):
                cor_copy(v, h, 0, v, h).wait_send()

    def send_share(total, par):
        m = jnp.where(lane1 < 64, jnp.broadcast_to(total, (1, 128)), fsum[...])
        asend[...] = m
        arecv[par, j] = m
        for o in range(1, ngy):
            share_copy(o, par, j).start()

    def row_fog(par):
        for o in range(1, ngy):
            share_copy(o, par, lax.rem(j + o, ngy)).wait_recv()
        total = jnp.zeros((nj, 128), F32)
        before = gbuf[1]
        for s in range(ngy):
            m = jnp.where(lane1 < 64, 1.0, -before[s // per : s // per + 1, :])
            total = total + qc[s] * (arecv[par, s] * m)
        r = total + pltpu.roll(total, 64, 1)
        bsend[...] = r
        brecv[par, i] = r
        for o in range(1, ngx):
            fog_copy(o, par, i).start()

    def get_fog(par):
        for o in range(1, ngx):
            fog_copy(o, par, lax.rem(i + o, ngx)).wait_recv()
        for a in range(3):
            row = jnp.clip(i - 1 + a, 0, ni - 1)
            weight = pc[row]
            total = jnp.zeros((nj, 128), F32)
            for s in range(ngx):
                total = total + weight[s : s + 1, :] * brecv[par, s]
            gbuf[a] = total

    def fog_at(a, col):
        return gbuf[a, pl.ds(col, 1), :]

    def blur_inner(par, last):
        def block(r):
            rows = slice(r * RB, r * RB + RB)
            now = d[rows, center]
            change = 0.75 - 0.75 * (f[rows, center] * now) - first_dot(r, pick_center)
            if last:
                out_r[rows, center] = change
            else:
                d[rows, center] = now + change

        for r in range(nb):
            rows = block_rows(r)
            for t in range(nt):
                put_main(rows, t, second_dot(chi[rows, :], clo[rows, :], t))
        for r in range(1, nb - 1):
            block(r)
        halo = []
        for v in range(2):
            row_copy(v, par, v).wait_recv()
        for v in range(2):
            halo.append(split(jnp.where(has_x[v], rrecv[par, v], 0.0)))
        hi = jnp.concatenate([halo[0][0], halo[1][0]], axis=0)
        lo = jnp.concatenate([halo[0][1], halo[1][1]], axis=0)
        for t in range(nt):
            x = second_dot(hi, lo, t)
            put_main(slice(0, PAD), t, x[:PAD])
            put_main(slice(PAD + height, 2 * PAD + height), t, x[PAD:])
        for r in (0, nb - 1):
            block(r)

    def fog_rows(r, x, cs):
        n = (cs.stop - cs.start) // 128
        if r == 0:
            first = x[:PAD] + wide(fog_at(0, blk_j), n) * uh[0, :, cs]
            return jnp.concatenate([first, x[PAD:]], axis=0)
        if r == nb - 1:
            final = x[RB - PAD :] + wide(fog_at(2, blk_j), n) * uh[1, :, cs]
            return jnp.concatenate([x[: RB - PAD], final], axis=0)
        return x

    def get_corners(v, par):
        sides = []
        for h in range(2):
            x = krecv[par, v, h] - fog_at(2 * v, side_j[h]) * fke[v, h]
            sides.append(unpack(jnp.where(has_x[v] & has_y[h], x, 0.0), 32 * h))
        return mix_ends(sides[0], sides[1])

    def get_columns(r, par):
        sides = []
        for h in range(2):
            x = crecv[par, h, r] - fog_at(1, side_j[h]) * fce[h, r]
            sides.append(unpack(jnp.where(has_y[h], x, 0.0), 32 * h))
        return mix_ends(sides[0], sides[1])

    def put_ends(first, mix):
        rows = slice(first, first + mix.shape[0])
        x = we[rows, :] + jnp.dot(jnp.concatenate([mix, mix], axis=1), wh[...], preferred_element_type=F32)
        put_blur(rows, left, x[:, :128])
        put_blur(rows, right, x[:, 128:])

    def blur_ends(par, use):
        half = nb // 2
        for h in range(2):
            cor_copy(0, h, par, 0, h).wait_recv()
            for r in range(half + 1):
                col_copy(h, r, par, h).wait_recv()
        for r in range(nb):
            sent_edges(r)
        put_ends(0, get_corners(0, par))
        for r in range(half + 1):
            put_ends(PAD + r * RB, get_columns(r, par))
        use([(r, first_dot(r, pick_ends)) for r in range(half)])
        for h in range(2):
            cor_copy(1, h, par, 1, h).wait_recv()
            for r in range(half + 1, nb):
                col_copy(h, r, par, h).wait_recv()
        for r in range(half + 1, nb):
            put_ends(PAD + r * RB, get_columns(r, par))
        put_ends(PAD + height, get_corners(1, par))
        use([(r, first_dot(r, pick_ends)) for r in range(half, nb)])

    def advance(k, carry):
        par = k % 2 if isinstance(k, int) else lax.rem(k, 2)
        nxt = 1 - par
        blur_inner(par, False)
        get_fog(1 - par)

        own = fog_at(1, blk_j)
        for r in range(nb):
            rows = slice(r * RB, r * RB + RB)
            new = d[rows, center] + wide(own, (breadth - 256) // 128) * w[rows, center]
            new = fog_rows(r, new, center)
            d[rows, center] = new
            x = f[rows, center] * new
            put_charge(r, center, x)
            add_acc(r, center, x)

        def use(backs):
            for r, back in backs:
                rows = slice(r * RB, r * RB + RB)
                sides = []
                for h in range(2):
                    cs = slice(edge[h], edge[h] + 128)
                    now = d[rows, cs]
                    cov = f[rows, cs]
                    new = now + (0.75 - 0.75 * (cov * now) - back[:, 128 * h : 128 * h + 128])
                    new = fog_rows(r, new + own * w[rows, cs], cs)
                    d[rows, cs] = new
                    x = cov * new
                    put_charge(r, cs, x)
                    add_acc(r, cs, x)
                    sides.append(x)
                fill_edges(r, sides, f[rows, center] * d[rows, center])
            for r, _ in backs:
                start_edges(r, nxt)

        blur_ends(par, use)
        for o in range(1, ngx):
            fog_copy(o, par, i).wait_send()
        row_fog(par)
        for o in range(1, ngy):
            share_copy(o, par, j).wait_send()
        send_share(reduce_acc(), nxt)
        return carry

    def own_halo_coverage():
        for v in range(2):
            frow_copy(v, v).wait_recv()
            fcol_copy(v, v).wait_recv()
            for h in range(2):
                fcor_copy(v, h, v, h).wait_recv()
        fce[...] = fcr[...]
        fke[...] = fkr[...]
        halo = jnp.concatenate([jnp.where(has_x[v], frr[v], 0.0) for v in range(2)], axis=0).astype(BF)
        for t in range(nt):
            hi, lo = split(second_dot(halo, jnp.zeros_like(halo), t))
            for v in range(2):
                part = slice(v * PAD, v * PAD + PAD)
                terms = jnp.concatenate([hi[part], hi[part], lo[part], jnp.zeros((PAD, CB), BF)], axis=0)
                uh[v, :, t * CB : t * CB + CB] = jnp.dot(ah[v], terms, preferred_element_type=F32)

    loads = []
    for r in range(nb):
        rows = pl.ds(r * RB, RB)
        loads.append((pltpu.make_async_copy(cover_hbm.at[rows], cover.at[rows], in_sem.at[0, r]),
                      pltpu.make_async_copy(dose_hbm.at[rows], d.at[rows], in_sem.at[1, r])))
        for c in loads[r]:
            c.start()
    pairs = ((a1_hbm, a1), (w2_hbm, w2), (wh_hbm, wh), (ah_hbm, ah), (qc_hbm, qc), (pc_hbm, pc))
    consts = [pltpu.make_async_copy(s, t, in_sem.at[2, n]) for n, (s, t) in enumerate(pairs)]
    for c in consts:
        c.start()

    barrier = pltpu.get_barrier_semaphore()
    partners = [dev(step_x[v], step_y[h]) for v in range(2) for h in range(2)]
    partners += [dev(i, lax.rem(j + o, ngy)) for o in range(1, ngy)]
    partners += [dev(lax.rem(i + o, ngx), j) for o in range(1, ngx)]
    for p in partners:
        pl.semaphore_signal(barrier, inc=1, device_id=p, device_id_type=MESH)

    bsend[...] = jnp.zeros_like(bsend)
    brecv[1, i] = jnp.zeros(bsend.shape, F32)
    uh[...] = jnp.zeros_like(uh)
    fce[...] = jnp.zeros_like(fce)
    fke[...] = jnp.zeros_like(fke)
    clo[...] = jnp.zeros_like(clo)
    for ref in (whi, wlo):
        ref[0:PAD, :] = jnp.zeros((PAD, breadth), BF)
        ref[PAD + height :, :] = jnp.zeros((PAD, breadth), BF)

    total = jnp.zeros((8, breadth), F32)
    for r in range(nb):
        rows = slice(r * RB, r * RB + RB)
        for c in loads[r]:
            c.wait()
        cov = cover[rows, :].astype(F32) * (1.0 / 64.0)
        f[rows, :] = cov
        total = total + fold(cov)
        chi[PAD + r * RB : PAD + r * RB + RB, :] = cov.astype(BF)
        for h in range(2):
            fcs[h, r] = pack(cov[:, edge[h] : edge[h] + 128], 96 * h)
            if r == 0:
                fks[0, h] = pack(cov[:PAD, edge[h] : edge[h] + 128], 96 * h)
            if r == nb - 1:
                fks[1, h] = pack(cov[RB - PAD :, edge[h] : edge[h] + 128], 96 * h)
        x = cov * d[rows, :]
        add_acc(r, slice(0, breadth), x)
        fill_edges(r, (x[:, left], x[:, right]), x[:, center])
    fsum[...] = jnp.broadcast_to(
        jnp.sum(jnp.sum(total, axis=0, keepdims=True), axis=1, keepdims=True), (1, 128))
    share = reduce_acc()

    for c in consts:
        c.wait()
    for r in range(nb):
        rows = block_rows(r)
        for t in range(nt):
            put_blur(rows, slice(t * CB, t * CB + CB), second_dot(chi[rows, :], clo[rows, :], t))
    for r in range(nb):
        rows = slice(r * RB, r * RB + RB)
        for t in range(nt):
            cs = slice(t * CB, t * CB + CB)
            u = first_dot(r, lambda ref, win: ref[win, cs])
            w[rows, cs] = u + 0.75 * f[rows, cs] - 1.0

    pl.semaphore_wait(barrier, len(partners))
    for r in range(nb):
        start_edges(r, 0)
    send_share(share, 0)
    for o in range(1, ngx):
        fog_copy(o, 1, i).start()
    for v in range(2):
        frow_copy(v, 1 - v).start()
        fcol_copy(v, into[v]).start()
        for h in range(2):
            fcor_copy(v, h, 1 - v, into[h]).start()
    for r in range(nb):
        rows = slice(r * RB, r * RB + RB)
        put_charge(r, slice(0, breadth), f[rows, :] * d[rows, :])

    advance(0, 0)
    own_halo_coverage()
    lax.fori_loop(1, ITERS - 1, advance, 0)

    par = (ITERS - 1) % 2
    blur_inner(par, True)
    get_fog(1 - par)
    own = fog_at(1, blk_j)
    for r in range(nb):
        rows = slice(r * RB, r * RB + RB)
        now = d[rows, center] - wide(own, (breadth - 256) // 128)
        change = out_r[rows, center] + wide(own, (breadth - 256) // 128) * (w[rows, center] + 1.0)
        change = fog_rows(r, change, center)
        d[rows, center] = now
        out_r[rows, center] = change

    def use_last(backs):
        for r, back in backs:
            rows = slice(r * RB, r * RB + RB)
            for h in range(2):
                cs = slice(edge[h], edge[h] + 128)
                now = d[rows, cs]
                change = 0.75 - 0.75 * (f[rows, cs] * now) - back[:, 128 * h : 128 * h + 128]
                change = change + own * (w[rows, cs] + 1.0)
                d[rows, cs] = now - own
                out_r[rows, cs] = fog_rows(r, change, cs)

    blur_ends(par, use_last)
    for o in range(1, ngx):
        fog_copy(o, par, i).wait_send()
    row_fog(par)
    get_fog(par)
    last = wide(fog_at(1, blk_j), breadth // 128)
    for r in range(nb):
        rows = slice(r * RB, r * RB + RB)
        change = out_r[rows, :] - last
        d[rows, :] = d[rows, :] + change
        out_r[rows, :] = change * (1.0 / 1.5)
    for v in range(2):
        frow_copy(v, v).wait_send()
        fcol_copy(v, v).wait_send()
        for h in range(2):
            fcor_copy(v, h, v, h).wait_send()
    for o in range(1, ngy):
        share_copy(o, par, j).wait_send()
    for o in range(1, ngx):
        fog_copy(o, par, i).wait_send()


def per_device(ngx, ngy, coverage, dose):
    height, breadth = dose.shape
    nb = height // RB
    ni, nj = ngx * height // COARSE, ngy * breadth // COARSE
    per = COARSE // breadth
    spread_j = fog_matrix(nj) / float(COARSE * COARSE)
    qc = np.stack([np.broadcast_to(spread_j[:, s // per, None], (nj, 128)) for s in range(ngy)])
    pc = np.broadcast_to(0.225 * fog_matrix(ni)[:, :, None], (ni, ni, 128))
    a1, w2, wh, ah = band_first(), band_second(), band_halo(breadth), band_rows()
    dma = pltpu.SemaphoreType.DMA
    vm = pltpu.VMEM
    any_spec = pl.BlockSpec(memory_space=pltpu.HBM)
    tile, padded = (height, breadth), (height + 2 * PAD, breadth)
    rows, cols, corners = (2, PAD, breadth), (2, nb, RB // 4, 128), (2, 2, PAD // 4, 128)
    return pl.pallas_call(
        functools.partial(kernel, ngx, ngy),
        out_shape=(vm(tile, F32), vm(tile, F32)),
        in_specs=[any_spec] * 8,
        out_specs=(pl.BlockSpec(memory_space=vm), pl.BlockSpec(memory_space=vm)),
        scratch_shapes=[
            vm(tile, jnp.int32), vm(tile, F32), vm(tile, F32),
            vm(a1.shape, BF), vm(w2.shape, BF), vm(wh.shape, BF), vm(ah.shape, BF), vm(qc.shape, F32), vm(pc.shape, F32),
            vm(padded, BF), vm(padded, BF), vm(padded, BF), vm(padded, BF), vm((height + 2 * PAD, 256), F32),
            vm((8, breadth), F32), vm((3, nj, 128), F32), vm((1, 128), F32), vm(rows, F32),
            vm(rows, F32), vm((2,) + rows, F32), vm(cols, F32), vm((2,) + cols, F32),
            vm(corners, F32), vm((2,) + corners, F32),
            vm(rows, F32), vm(cols, F32), vm(cols, F32), vm(corners, F32), vm(corners, F32),
            vm(cols, F32), vm(corners, F32),
            vm((1, 128), F32), vm((2, ngy, 1, 128), F32), vm((nj, 128), F32), vm((2, ngx, nj, 128), F32),
            dma((3, max(nb, 6))),
            dma((2,)), dma((2, 2)), dma((2, nb)), dma((2, 2, nb)), dma((2, 2)), dma((2, 2, 2)),
            dma((2,)), dma((2,)), dma((2,)), dma((2,)), dma((2, 2)), dma((2, 2)),
            dma((ngy,)), dma((2, ngy)), dma((ngx,)), dma((2, ngx)),
        ],
        compiler_params=pltpu.CompilerParams(
            collective_id=0, has_side_effects=True, vmem_limit_bytes=52 * 2**20
        ),
    )(coverage, dose, jnp.asarray(a1), jnp.asarray(w2), jnp.asarray(wh), jnp.asarray(ah),
      jnp.asarray(qc, F32), jnp.asarray(pc, F32))


def solution(mesh):
    return jax.shard_map(
        functools.partial(per_device, mesh.shape["gx"], mesh.shape["gy"]),
        mesh=mesh,
        in_specs=(P("gx", "gy"), P("gx", "gy")),
        out_specs=(P("gx", "gy"), P("gx", "gy")),
        check_vma=False,
    )
```

```python
import functools
import math

import jax
import jax.numpy as jnp
import numpy as np
from jax import lax
from jax.experimental import pallas as pl
from jax.experimental.pallas import tpu as pltpu
from jax.sharding import PartitionSpec as P

RIM = 30
PAD = 32
COARSE = 1024
FOG = 3072
ITERS = 6
RB = 256
CB = 256
KW = RB + 2 * PAD
BF = jnp.bfloat16
F32 = jnp.float32
MESH = pl.DeviceIdType.MESH


def two_terms(x):
    hi = np.asarray(x, np.float32).astype(BF)
    lo = (x - hi.astype(np.float64)).astype(np.float32).astype(BF)
    return hi, lo


def taps():
    k = np.arange(-RIM, RIM + 1).astype(np.float64)
    w = np.exp(-k * k / 200.0)
    return w / w.sum()


def band_first():
    w = taps()
    band = np.zeros((RB, KW))
    for i in range(RB):
        band[i, i + PAD - RIM : i + PAD + RIM + 1] = w
    hi, lo = two_terms(band)
    return np.concatenate([hi, lo, hi], axis=1)


def band_rows():
    w = taps()
    out = []
    for offset in (-PAD, PAD):
        band = np.array([[w[m + offset - i + RIM] if abs(m + offset - i) <= RIM else 0.0
                          for m in range(PAD)] for i in range(PAD)])
        hi, lo = two_terms(band)
        out.append(np.concatenate([hi, lo, hi, np.zeros_like(hi)], axis=1))
    return np.stack(out)


def second_weights(columns, outputs):
    w = 0.525 * taps()
    return np.array([[w[c - j + RIM] if abs(c - j) <= RIM else 0.0 for j in outputs] for c in columns])


def band_second():
    out = []
    for beside in (range(CB, CB + 128), range(-128, 0)):
        mh, ml = two_terms(second_weights(range(CB), range(CB)))
        xh, xl = two_terms(second_weights(beside, range(CB)))
        out.append(np.concatenate([mh, ml, mh, xh, xl, xh], axis=0))
    return np.stack(out)


def band_halo(breadth):
    columns = list(range(-PAD, 0)) + list(range(breadth, breadth + PAD))
    outputs = list(range(128)) + list(range(breadth - 128, breadth))
    hi, lo = two_terms(second_weights(columns, outputs))
    return np.concatenate([hi, hi, lo, lo], axis=0)


def fog_matrix(n):
    s = FOG / COARSE
    k = np.arange(n).astype(np.float64)
    spread = k[:, None] - k[None, :]
    return np.exp(-spread * spread / (2.0 * s * s)) / (math.sqrt(2.0 * math.pi) * s)


def split(x):
    hi = x.astype(BF)
    return hi, (x - hi.astype(F32)).astype(BF)


def wide(row, n):
    return jnp.concatenate([row] * n, axis=1)


def kernel(ngx, ngy, cover_hbm, dose_hbm, a1_hbm, w2_hbm, wh_hbm, ah_hbm, qc_hbm, pc_hbm, d, out_r, out_g,
           cover, f, w, a1, w2, wh, ah, qc, pc, chi, clo, whi, wlo, we, acc, gbuf, fsum, uh,
           rsend, rrecv, csend, crecv, ksend, krecv, frr, fcs, fcr, fks, fkr, fce, fke,
           asend, arecv, bsend, brecv,
           in_sem, row_s, row_r, col_s, col_r, cor_s, cor_r,
           frow_s, frow_r, fcol_s, fcol_r, fcor_s, fcor_r, fa_s, fa_r, fb_s, fb_r):
    height, breadth = d.shape
    nb = height // RB
    nt = breadth // CB
    per = COARSE // breadth
    ni, nj = ngx * height // COARSE, ngy * breadth // COARSE
    i, j = lax.axis_index("gx"), lax.axis_index("gy")
    step_x = (lax.rem(i + ngx - 1, ngx), lax.rem(i + 1, ngx))
    has_x = (i > 0, i < ngx - 1)
    has_y = (j > 0, j < ngy - 1)
    step_y = (jnp.maximum(j - 1, 0), jnp.minimum(j + 1, ngy - 1))
    beside = tuple(jnp.where(has_y[h], i, i + 1 - 2 * lax.rem(i, 2)) for h in range(2))
    into = tuple(jnp.where(has_y[h], 1 - h, h) for h in range(2))
    blk_j = j // per
    side_j = (step_y[0] // per, step_y[1] // per)
    edge = (0, breadth - 128)
    center = slice(128, breadth - 128)
    left, right = slice(0, 128), slice(breadth - 128, breadth)

    def dev(x, y):
        return {"gx": x, "gy": y}

    def remote(src, dst, ss, rs, to):
        return pltpu.make_async_remote_copy(
            src_ref=src, dst_ref=dst, send_sem=ss, recv_sem=rs, device_id=to, device_id_type=MESH
        )

    def row_copy(v, par, slot):
        return remote(rsend.at[v], rrecv.at[par, slot], row_s.at[v], row_r.at[par, slot], dev(step_x[v], j))

    def col_copy(h, r, par, slot):
        return remote(csend.at[h, r], crecv.at[par, slot, r], col_s.at[h, r], col_r.at[par, slot, r],
                      dev(beside[h], step_y[h]))

    def cor_copy(v, h, par, sv, sh):
        return remote(ksend.at[v, h], krecv.at[par, sv, sh], cor_s.at[v, h], cor_r.at[par, sv, sh],
                      dev(step_x[v], step_y[h]))

    def frow_copy(v, slot):
        return remote(f.at[pl.ds(v * (height - PAD), PAD)], frr.at[slot], frow_s.at[v], frow_r.at[slot],
                      dev(step_x[v], j))

    def fcol_copy(h, slot):
        return remote(fcs.at[h], fcr.at[slot], fcol_s.at[h], fcol_r.at[slot], dev(beside[h], step_y[h]))

    def fcor_copy(v, h, sv, sh):
        return remote(fks.at[v, h], fkr.at[sv, sh], fcor_s.at[v, h], fcor_r.at[sv, sh],
                      dev(step_x[v], step_y[h]))

    def share_copy(o, par, slot):
        return remote(asend, arecv.at[par, slot], fa_s.at[o], fa_r.at[par, slot],
                      dev(i, lax.rem(j + o, ngy)))

    def fog_copy(o, par, slot):
        return remote(bsend, brecv.at[par, slot], fb_s.at[o], fb_r.at[par, slot],
                      dev(lax.rem(i + o, ngx), j))

    lane1 = lax.broadcasted_iota(jnp.int32, (1, 128), 1)

    def lanes(n):
        return lax.broadcasted_iota(jnp.int32, (n, 128), 1)

    def roll(x, shift):
        shift = shift % 128
        return x if shift == 0 else pltpu.roll(x, shift, 1)

    def pack(tile, first_lane):
        n = tile.shape[0] // 4
        lane = lanes(n)
        parts = [roll(tile[n * q : n * q + n], 32 * q - first_lane) for q in range(4)]
        low = jnp.where(lane < 32, parts[0], parts[1])
        high = jnp.where(lane < 96, parts[2], parts[3])
        return jnp.where(lane < 64, low, high)

    def unpack(piece, first_lane):
        return jnp.concatenate([roll(piece, first_lane - 32 * q) for q in range(4)], axis=0)

    def mix_ends(low, high):
        lane = lanes(low.shape[0])
        e = jnp.where(lane < 32, low, high)
        e = jnp.where(lane < 64, e, roll(e, 64))
        hi = e.astype(BF).astype(F32)
        return jnp.where(lane < 64, hi, e - hi).astype(BF)

    def put_charge(r, cs, x):
        hi, lo = split(x)
        chi[PAD + r * RB : PAD + r * RB + RB, cs] = hi
        clo[PAD + r * RB : PAD + r * RB + RB, cs] = lo

    def put_blur(rows, cs, x):
        hi, lo = split(x)
        whi[rows, cs] = hi
        wlo[rows, cs] = lo

    def put_main(rows, t, x):
        if t == 0:
            we[rows, 0:128] = x[:, :128]
            put_blur(rows, slice(128, CB), x[:, 128:])
        else:
            put_blur(rows, slice(CB, breadth - 128), x[:, :128])
            we[rows, 128:256] = x[:, 128:]

    def first_dot(r, pick):
        rows = slice(r * RB, r * RB + KW)
        hi = pick(whi, rows)
        return jnp.dot(a1[...], jnp.concatenate([hi, hi, pick(wlo, rows)], axis=0),
                       preferred_element_type=F32)

    def pick_center(ref, rows):
        return ref[rows, center]

    def pick_ends(ref, rows):
        return jnp.concatenate([ref[rows, left], ref[rows, right]], axis=1)

    def second_dot(hi, lo, t):
        own = slice(t * CB, t * CB + CB)
        other = slice(CB, CB + 128) if t == 0 else slice(CB - 128, CB)
        lhs = jnp.concatenate(
            [hi[:, own], hi[:, own], lo[:, own], hi[:, other], hi[:, other], lo[:, other]], axis=1)
        return jnp.dot(lhs, w2[t], preferred_element_type=F32)

    def block_rows(r):
        return slice(PAD + r * RB, PAD + r * RB + RB)

    def fold(x):
        return jnp.sum(x.reshape(x.shape[0] // 8, 8, x.shape[1]), axis=0)

    def add_acc(r, cs, x):
        acc[:, cs] = fold(x) if r == 0 else acc[:, cs] + fold(x)

    def reduce_acc():
        return jnp.sum(jnp.sum(acc[...], axis=0, keepdims=True), axis=1, keepdims=True)

    def fill_edges(r, sides, mids):
        for h in range(2):
            csend[h, r] = pack(sides[h], 96 * h)
        if r == 0 or r == nb - 1:
            v = 0 if r == 0 else 1
            part = slice(0, PAD) if v == 0 else slice(RB - PAD, RB)
            rsend[v, :, left] = sides[0][part]
            rsend[v, :, right] = sides[1][part]
            rsend[v, :, center] = mids[part]
            for h in range(2):
                ksend[v, h] = pack(sides[h][part], 96 * h)

    def start_columns(r, par):
        for h in range(2):
            col_copy(h, r, par, into[h]).start()

    def start_rows(r, par):
        if r == 0 or r == nb - 1:
            v = 0 if r == 0 else 1
            row_copy(v, par, 1 - v).start()
            for h in range(2):
                cor_copy(v, h, par, 1 - v, into[h]).start()

    def sent_edges(r):
        for h in range(2):
            col_copy(h, r, 0, h).wait_send()
        if r == 0 or r == nb - 1:
            v = 0 if r == 0 else 1
            row_copy(v, 0, v).wait_send()
            for h in range(2):
                cor_copy(v, h, 0, v, h).wait_send()

    def send_share(total, par):
        m = jnp.where(lane1 < 64, jnp.broadcast_to(total, (1, 128)), fsum[...])
        asend[...] = m
        arecv[par, j] = m
        for o in range(1, ngy):
            share_copy(o, par, j).start()

    def row_fog(par):
        for o in range(1, ngx):
            fog_copy(o, par, i).wait_send()
        for o in range(1, ngy):
            share_copy(o, par, lax.rem(j + o, ngy)).wait_recv()
        total = jnp.zeros((nj, 128), F32)
        before = gbuf[1]
        for s in range(ngy):
            m = jnp.where(lane1 < 64, 1.0, -before[s // per : s // per + 1, :])
            total = total + qc[s] * (arecv[par, s] * m)
        r = total + pltpu.roll(total, 64, 1)
        bsend[...] = r
        brecv[par, i] = r
        for o in range(1, ngx):
            fog_copy(o, par, i).start()

    def get_fog(par):
        for o in range(1, ngx):
            fog_copy(o, par, lax.rem(i + o, ngx)).wait_recv()
        for a in range(3):
            row = jnp.clip(i - 1 + a, 0, ni - 1)
            weight = pc[row]
            total = jnp.zeros((nj, 128), F32)
            for s in range(ngx):
                total = total + weight[s : s + 1, :] * brecv[par, s]
            gbuf[a] = total

    def fog_at(a, col):
        return gbuf[a, pl.ds(col, 1), :]

    def blur_inner(par, last):
        def block(r):
            rows = slice(r * RB, r * RB + RB)
            now = d[rows, center]
            change = 0.75 - 0.75 * (f[rows, center] * now) - first_dot(r, pick_center)
            if last:
                out_r[rows, center] = change
            else:
                d[rows, center] = now + change

        for r in range(nb):
            rows = block_rows(r)
            for t in range(nt):
                put_main(rows, t, second_dot(chi[rows, :], clo[rows, :], t))
        for r in range(1, nb - 1):
            block(r)
        halo = []
        for v in range(2):
            row_copy(v, par, v).wait_recv()
        for v in range(2):
            halo.append(split(jnp.where(has_x[v], rrecv[par, v], 0.0)))
        hi = jnp.concatenate([halo[0][0], halo[1][0]], axis=0)
        lo = jnp.concatenate([halo[0][1], halo[1][1]], axis=0)
        for t in range(nt):
            x = second_dot(hi, lo, t)
            put_main(slice(0, PAD), t, x[:PAD])
            put_main(slice(PAD + height, 2 * PAD + height), t, x[PAD:])
        for r in (0, nb - 1):
            block(r)

    def fog_rows(r, x, cs):
        n = (cs.stop - cs.start) // 128
        if r == 0:
            first = x[:PAD] + wide(fog_at(0, blk_j), n) * uh[0, :, cs]
            return jnp.concatenate([first, x[PAD:]], axis=0)
        if r == nb - 1:
            final = x[RB - PAD :] + wide(fog_at(2, blk_j), n) * uh[1, :, cs]
            return jnp.concatenate([x[: RB - PAD], final], axis=0)
        return x

    def get_corners(v, par):
        sides = []
        for h in range(2):
            x = krecv[par, v, h] - fog_at(2 * v, side_j[h]) * fke[v, h]
            sides.append(unpack(jnp.where(has_x[v] & has_y[h], x, 0.0), 32 * h))
        return mix_ends(sides[0], sides[1])

    def get_columns(r, par):
        sides = []
        for h in range(2):
            x = crecv[par, h, r] - fog_at(1, side_j[h]) * fce[h, r]
            sides.append(unpack(jnp.where(has_y[h], x, 0.0), 32 * h))
        return mix_ends(sides[0], sides[1])

    def put_ends(first, mix):
        rows = slice(first, first + mix.shape[0])
        x = we[rows, :] + jnp.dot(jnp.concatenate([mix, mix], axis=1), wh[...], preferred_element_type=F32)
        put_blur(rows, left, x[:, :128])
        put_blur(rows, right, x[:, 128:])

    def blur_ends(par, use, between):
        half = nb // 2
        for h in range(2):
            cor_copy(0, h, par, 0, h).wait_recv()
            for r in range(half + 1):
                col_copy(h, r, par, h).wait_recv()
        for r in range(nb):
            sent_edges(r)
        put_ends(0, get_corners(0, par))
        for r in range(half + 1):
            put_ends(PAD + r * RB, get_columns(r, par))
        use([(r, first_dot(r, pick_ends)) for r in range(half)])
        between()
        for h in range(2):
            cor_copy(1, h, par, 1, h).wait_recv()
            for r in range(half + 1, nb):
                col_copy(h, r, par, h).wait_recv()
        for r in range(half + 1, nb):
            put_ends(PAD + r * RB, get_columns(r, par))
        put_ends(PAD + height, get_corners(1, par))
        use([(r, first_dot(r, pick_ends)) for r in range(half, nb)])

    def advance(k, carry):
        par = k % 2 if isinstance(k, int) else lax.rem(k, 2)
        nxt = 1 - par
        blur_inner(par, False)
        get_fog(1 - par)

        own = fog_at(1, blk_j)
        for r in range(nb):
            rows = slice(r * RB, r * RB + RB)
            new = d[rows, center] + wide(own, (breadth - 256) // 128) * w[rows, center]
            new = fog_rows(r, new, center)
            d[rows, center] = new
            x = f[rows, center] * new
            put_charge(r, center, x)
            add_acc(r, center, x)

        def use(backs):
            for r, back in backs:
                rows = slice(r * RB, r * RB + RB)
                sides = []
                for h in range(2):
                    cs = slice(edge[h], edge[h] + 128)
                    now = d[rows, cs]
                    cov = f[rows, cs]
                    new = now + (0.75 - 0.75 * (cov * now) - back[:, 128 * h : 128 * h + 128])
                    new = fog_rows(r, new + own * w[rows, cs], cs)
                    d[rows, cs] = new
                    x = cov * new
                    put_charge(r, cs, x)
                    add_acc(r, cs, x)
                    sides.append(x)
                fill_edges(r, sides, f[rows, center] * d[rows, center])
            for r, _ in backs:
                start_columns(r, nxt)
            for r, _ in backs:
                start_rows(r, nxt)

        blur_ends(par, use, lambda: row_fog(par))
        for o in range(1, ngy):
            share_copy(o, par, j).wait_send()
        send_share(reduce_acc(), nxt)
        return carry

    def own_halo_coverage():
        for v in range(2):
            frow_copy(v, v).wait_recv()
            fcol_copy(v, v).wait_recv()
            for h in range(2):
                fcor_copy(v, h, v, h).wait_recv()
        fce[...] = fcr[...]
        fke[...] = fkr[...]
        halo = jnp.concatenate([jnp.where(has_x[v], frr[v], 0.0) for v in range(2)], axis=0).astype(BF)
        for t in range(nt):
            hi, lo = split(second_dot(halo, jnp.zeros_like(halo), t))
            for v in range(2):
                part = slice(v * PAD, v * PAD + PAD)
                terms = jnp.concatenate([hi[part], hi[part], lo[part], jnp.zeros((PAD, CB), BF)], axis=0)
                uh[v, :, t * CB : t * CB + CB] = jnp.dot(ah[v], terms, preferred_element_type=F32)

    loads = []
    for r in range(nb):
        rows = pl.ds(r * RB, RB)
        loads.append((pltpu.make_async_copy(cover_hbm.at[rows], cover.at[rows], in_sem.at[0, r]),
                      pltpu.make_async_copy(dose_hbm.at[rows], d.at[rows], in_sem.at[1, r])))
        for c in loads[r]:
            c.start()
    pairs = ((a1_hbm, a1), (w2_hbm, w2), (wh_hbm, wh), (ah_hbm, ah), (qc_hbm, qc), (pc_hbm, pc))
    consts = [pltpu.make_async_copy(s, t, in_sem.at[2, n]) for n, (s, t) in enumerate(pairs)]
    for c in consts:
        c.start()

    barrier = pltpu.get_barrier_semaphore()
    partners = [dev(step_x[v], step_y[h]) for v in range(2) for h in range(2)]
    partners += [dev(i, lax.rem(j + o, ngy)) for o in range(1, ngy)]
    partners += [dev(lax.rem(i + o, ngx), j) for o in range(1, ngx)]
    for p in partners:
        pl.semaphore_signal(barrier, inc=1, device_id=p, device_id_type=MESH)

    bsend[...] = jnp.zeros_like(bsend)
    brecv[1, i] = jnp.zeros(bsend.shape, F32)
    uh[...] = jnp.zeros_like(uh)
    fce[...] = jnp.zeros_like(fce)
    fke[...] = jnp.zeros_like(fke)
    clo[...] = jnp.zeros_like(clo)
    for ref in (whi, wlo):
        ref[0:PAD, :] = jnp.zeros((PAD, breadth), BF)
        ref[PAD + height :, :] = jnp.zeros((PAD, breadth), BF)

    total = jnp.zeros((8, breadth), F32)
    for r in range(nb):
        rows = slice(r * RB, r * RB + RB)
        for c in loads[r]:
            c.wait()
        cov = cover[rows, :].astype(F32) * (1.0 / 64.0)
        f[rows, :] = cov
        total = total + fold(cov)
        chi[PAD + r * RB : PAD + r * RB + RB, :] = cov.astype(BF)
        for h in range(2):
            fcs[h, r] = pack(cov[:, edge[h] : edge[h] + 128], 96 * h)
            if r == 0:
                fks[0, h] = pack(cov[:PAD, edge[h] : edge[h] + 128], 96 * h)
            if r == nb - 1:
                fks[1, h] = pack(cov[RB - PAD :, edge[h] : edge[h] + 128], 96 * h)
        x = cov * d[rows, :]
        add_acc(r, slice(0, breadth), x)
        fill_edges(r, (x[:, left], x[:, right]), x[:, center])
    fsum[...] = jnp.broadcast_to(
        jnp.sum(jnp.sum(total, axis=0, keepdims=True), axis=1, keepdims=True), (1, 128))
    share = reduce_acc()

    pl.semaphore_wait(barrier, len(partners))
    for r in range(nb):
        start_columns(r, 0)
        start_rows(r, 0)
    send_share(share, 0)
    for o in range(1, ngx):
        fog_copy(o, 1, i).start()
    for v in range(2):
        frow_copy(v, 1 - v).start()
        fcol_copy(v, into[v]).start()
        for h in range(2):
            fcor_copy(v, h, 1 - v, into[h]).start()
    for c in consts:
        c.wait()
    for r in range(nb):
        rows = block_rows(r)
        for t in range(nt):
            put_blur(rows, slice(t * CB, t * CB + CB), second_dot(chi[rows, :], clo[rows, :], t))
    for r in range(nb):
        rows = slice(r * RB, r * RB + RB)
        for t in range(nt):
            cs = slice(t * CB, t * CB + CB)
            u = first_dot(r, lambda ref, win: ref[win, cs])
            w[rows, cs] = u + 0.75 * f[rows, cs] - 1.0

    for r in range(nb):
        rows = slice(r * RB, r * RB + RB)
        put_charge(r, slice(0, breadth), f[rows, :] * d[rows, :])

    advance(0, 0)
    own_halo_coverage()
    lax.fori_loop(1, ITERS - 1, advance, 0)

    par = (ITERS - 1) % 2
    blur_inner(par, True)
    get_fog(1 - par)
    own = fog_at(1, blk_j)
    for r in range(nb):
        rows = slice(r * RB, r * RB + RB)
        now = d[rows, center] - wide(own, (breadth - 256) // 128)
        change = out_r[rows, center] + wide(own, (breadth - 256) // 128) * (w[rows, center] + 1.0)
        change = fog_rows(r, change, center)
        d[rows, center] = now
        out_r[rows, center] = change

    def use_last(backs):
        for r, back in backs:
            rows = slice(r * RB, r * RB + RB)
            for h in range(2):
                cs = slice(edge[h], edge[h] + 128)
                now = d[rows, cs]
                change = 0.75 - 0.75 * (f[rows, cs] * now) - back[:, 128 * h : 128 * h + 128]
                change = change + own * (w[rows, cs] + 1.0)
                d[rows, cs] = now - own
                out_r[rows, cs] = fog_rows(r, change, cs)

    row_fog(par)
    blur_ends(par, use_last, lambda: None)
    get_fog(par)
    out_g[...] = fog_at(1, blk_j)
    for v in range(2):
        frow_copy(v, v).wait_send()
        fcol_copy(v, v).wait_send()
        for h in range(2):
            fcor_copy(v, h, v, h).wait_send()
    for o in range(1, ngy):
        share_copy(o, par, j).wait_send()
    for o in range(1, ngx):
        fog_copy(o, par, i).wait_send()


def per_device(ngx, ngy, coverage, dose):
    height, breadth = dose.shape
    nb = height // RB
    ni, nj = ngx * height // COARSE, ngy * breadth // COARSE
    per = COARSE // breadth
    spread_j = fog_matrix(nj) / float(COARSE * COARSE)
    qc = np.stack([np.broadcast_to(spread_j[:, s // per, None], (nj, 128)) for s in range(ngy)])
    pc = np.broadcast_to(0.225 * fog_matrix(ni)[:, :, None], (ni, ni, 128))
    a1, w2, wh, ah = band_first(), band_second(), band_halo(breadth), band_rows()
    dma = pltpu.SemaphoreType.DMA
    vm = pltpu.VMEM
    any_spec = pl.BlockSpec(memory_space=pltpu.HBM)
    tile, padded = (height, breadth), (height + 2 * PAD, breadth)
    rows, cols, corners = (2, PAD, breadth), (2, nb, RB // 4, 128), (2, 2, PAD // 4, 128)
    dose_map, change, last = pl.pallas_call(
        functools.partial(kernel, ngx, ngy),
        out_shape=(vm(tile, F32), vm(tile, F32), vm((1, 128), F32)),
        in_specs=[any_spec] * 8,
        out_specs=(pl.BlockSpec(memory_space=vm),) * 3,
        scratch_shapes=[
            vm(tile, jnp.int32), vm(tile, F32), vm(tile, F32),
            vm(a1.shape, BF), vm(w2.shape, BF), vm(wh.shape, BF), vm(ah.shape, BF), vm(qc.shape, F32), vm(pc.shape, F32),
            vm(padded, BF), vm(padded, BF), vm(padded, BF), vm(padded, BF), vm((height + 2 * PAD, 256), F32),
            vm((8, breadth), F32), vm((3, nj, 128), F32), vm((1, 128), F32), vm(rows, F32),
            vm(rows, F32), vm((2,) + rows, F32), vm(cols, F32), vm((2,) + cols, F32),
            vm(corners, F32), vm((2,) + corners, F32),
            vm(rows, F32), vm(cols, F32), vm(cols, F32), vm(corners, F32), vm(corners, F32),
            vm(cols, F32), vm(corners, F32),
            vm((1, 128), F32), vm((2, ngy, 1, 128), F32), vm((nj, 128), F32), vm((2, ngx, nj, 128), F32),
            dma((3, max(nb, 6))),
            dma((2,)), dma((2, 2)), dma((2, nb)), dma((2, 2, nb)), dma((2, 2)), dma((2, 2, 2)),
            dma((2,)), dma((2,)), dma((2,)), dma((2,)), dma((2, 2)), dma((2, 2)),
            dma((ngy,)), dma((2, ngy)), dma((ngx,)), dma((2, ngx)),
        ],
        compiler_params=pltpu.CompilerParams(
            collective_id=0, has_side_effects=True, vmem_limit_bytes=52 * 2**20
        ),
    )(coverage, dose, jnp.asarray(a1), jnp.asarray(w2), jnp.asarray(wh), jnp.asarray(ah),
      jnp.asarray(qc, F32), jnp.asarray(pc, F32))
    change = change - last[0, 0]
    return dose_map + change, change * (1.0 / 1.5)


def solution(mesh):
    return jax.shard_map(
        functools.partial(per_device, mesh.shape["gx"], mesh.shape["gy"]),
        mesh=mesh,
        in_specs=(P("gx", "gy"), P("gx", "gy")),
        out_specs=(P("gx", "gy"), P("gx", "gy")),
        check_vma=False,
    )
```
